256 devices in a mesh: gz: 64 (over z_hi, y, x), gy: 4 (over z_lo, core).
Axes of the slice: x: 4, y: 4, z: 8 (z_hi: 4, z_lo: 2; z = z_hi * 2 + z_lo), core: 2. Of those that a mesh axis runs over, the one named last changes fastest.
Arguments:
- state: float32 [5, 512, 256, 256], P(None, 'gz', 'gy'), may hold values from -1.2 to 1.7, as said below
- adjoint_seed: float32 [5, 512, 256, 256], P(None, 'gz', 'gy'), may hold values from -15 to 15
- fluid_mask: int32 [512, 256, 256], P('gz', 'gy'), may hold values 0 or 1
- boundary_codes: int32 [512, 256], P('gz', 'gy'), may hold values from 0 to 3
Outputs:
- state_next: float32 [5, 512, 256, 256], P(None, 'gz', 'gy')
- gradient_direction: float32 [5, 512, 256, 256], P(None, 'gz', 'gy')
- gradient_gain: float32 [], replicated
The draws below stay inside these ranges and needn't reach their ends.
Inputs may be any that keep to these rules, and one draw needn't show every extreme that they name: `state`: component 0 is a density between 0.8 and 1.2; component 4 lies between 0 and the density.
All inputs are finite; a program needn't handle non-finite values. No bound on the sum of `fluid_mask` on one device may be relied on, other than what follows from the above.
Results may differ from the reference program's by a relative error of at most 0.019.
Values sent between devices are 32-bit elements; how exact they have to be, the bound alone decides.
A program may use at most 128 MiB of HBM per device.

```python
import jax
import jax.numpy as jnp
from jax import lax

CZ = 8
NX = 256
NZ = 512
NY = 256


def draw_state(key, part):
    key = jax.random.fold_in(key, 11)
    keys = jax.random.split(key, 3)
    shape = (NZ, NY, NX)
    streamwise = jnp.zeros((3, 1, 1, 1), jnp.float32).at[2].set(0.5)
    density = 1.0 + jax.random.uniform(keys[0], shape, jnp.float32, -0.15, 0.15)
    velocity = jnp.clip(0.3 * jax.random.normal(keys[1], (3,) + shape, jnp.float32), -0.9, 0.9) + streamwise
    fraction = jax.random.uniform(keys[2], shape, jnp.float32, 0.0, 1.0)
    return jnp.concatenate([density[None], density[None] * velocity, (density * fraction)[None]], 0)


def draw_adjoint_seed(key, part):
    key = jax.random.fold_in(key, 23)
    keys = jax.random.split(key, 2)
    shape = (5, NZ, NY, NX)
    ramp = 1.0 + 2.0 * jnp.arange(NZ, dtype=jnp.float32) / (NZ - 1)
    band_index = jnp.arange(NZ, dtype=jnp.int32) * 8 // NZ
    band_factor = jax.random.uniform(keys[1], (8,), jnp.float32, 1.0, 2.0)
    band_table = (band_index[:, None] == jnp.arange(8, dtype=jnp.int32)[None, :]).astype(jnp.float32)
    profile = ramp * jnp.sum(band_table * band_factor[None, :], axis=1)
    values = jnp.clip(jax.random.normal(keys[0], shape, jnp.float32), -2.5, 2.5)
    return values * profile[None, :, None, None]


def touch_ends(values, stream_key, smallest, largest):
    dims = values.shape
    index_at = [jax.random.randint(jax.random.fold_in(stream_key, axis), (), 0, dims[axis]) for axis in range(len(dims))]
    values = values.at[tuple(index_at)].set(smallest)
    longest = dims.index(max(dims))
    index_at[longest] = (index_at[longest] + 1) % dims[longest]
    return values.at[tuple(index_at)].set(largest)


def setup_inputs(seed: int = 0) -> dict:
    splits = jax.random.split(jax.random.key(seed), 5)
    return {
        "state": draw_state(jax.random.fold_in(splits[4], 71), 0),
        "adjoint_seed": draw_adjoint_seed(jax.random.fold_in(splits[4], 71), 0),
        "fluid_mask": touch_ends((jax.random.randint(splits[2], (NZ, NY, NX), 0, 8) < 7).astype(jnp.int32), jax.random.fold_in(splits[2], 1), 0, 1),
        "boundary_codes": touch_ends(jax.random.randint(splits[3], (NZ, NY), 0, 4), jax.random.fold_in(splits[3], 1), 0, 3).astype(jnp.int32),
    }


step_size = 0.25
sponge_table = (0.0, 0.5, 1.0, 2.0)
far_state = (1.0, 0.0, 0.0, 0.5, 0.0)

def flux(values, direction):
    density = values[0]
    velocity = values[1 + direction] / density
    pressure = (density ** 7 - 1.0) / 7.0
    pieces = [values[1 + direction]]
    for component in range(3):
        momentum_flux = values[1 + component] * velocity
        if component == direction:
            momentum_flux = momentum_flux + pressure
        pieces.append(momentum_flux)
    pieces.append(values[4] * velocity)
    return jnp.stack(pieces)

def adjoint(values, vector, direction):
    density = values[0]
    velocities = [values[1 + component] / density for component in range(3)]
    ratio = values[4] / density
    along_speed = velocities[direction]
    inner = velocities[0] * vector[1] + velocities[1] * vector[2] + velocities[2] * vector[3]
    back_density = -along_speed * inner + density ** 6 * vector[1 + direction] - ratio * along_speed * vector[4]
    pieces = [back_density]
    for component in range(3):
        back_momentum = along_speed * vector[1 + component]
        if component == direction:
            back_momentum = back_momentum + (vector[0] + inner + ratio * vector[4])
        pieces.append(back_momentum)
    pieces.append(along_speed * vector[4])
    return jnp.stack(pieces)

def central(padded, along, length):

    def window(offset):
        return lax.slice_in_dim(padded, 2 + offset, 2 + offset + length, axis=along)
    return (8.0 * (window(1) - window(-1)) - (window(2) - window(-2))) / 12.0

def sponge_of(boundary_codes):
    sponge = jnp.zeros(boundary_codes.shape, jnp.float32)
    for code_value, strength in enumerate(sponge_table):
        sponge = sponge + jnp.where(boundary_codes == code_value, strength, 0.0)
    return sponge

def reference(state, adjoint_seed, fluid_mask, boundary_codes):
    far = jnp.array(far_state, jnp.float32)[:, None, None, None]
    fluid_all = fluid_mask.astype(jnp.float32)
    weighted_all = step_size * fluid_all[None] * adjoint_seed
    padded_state = jnp.stack([jnp.pad(state[0], 2, constant_values=1.0)] + [jnp.pad(state[k], 2) for k in range(1, 5)])
    padded_seed = jnp.pad(weighted_all, ((0, 0), (2, 2), (2, 2), (2, 2)))
    inside_y = (jnp.abs(jnp.arange(NY + 4, dtype=jnp.int32) - 2 - (NY - 1) / 2.0) < NY / 2.0).astype(jnp.float32)
    inside_x = (jnp.abs(jnp.arange(NX + 4, dtype=jnp.int32) - 2 - (NX - 1) / 2.0) < NX / 2.0).astype(jnp.float32)

    def block(number):
        start = (number * CZ).astype(jnp.int32)
        rows_z = start + jnp.arange(CZ + 4, dtype=jnp.int32) - 2
        inside_z = ((rows_z >= 0) & (rows_z < NZ)).astype(jnp.float32)
        window_state = lax.dynamic_slice_in_dim(padded_state, start, CZ + 4, axis=1)
        window_seed = lax.dynamic_slice_in_dim(padded_seed, start, CZ + 4, axis=1)
        values = lax.dynamic_slice_in_dim(state, start, CZ, axis=1)
        seed_block = lax.dynamic_slice_in_dim(adjoint_seed, start, CZ, axis=1)
        fluid = lax.dynamic_slice_in_dim(fluid_all, start, CZ, axis=0)
        sponge = sponge_of(lax.dynamic_slice_in_dim(boundary_codes, start, CZ, axis=0))[None, :, :, None]
        flux_z = flux(window_state[:, :, 2:-2, 2:-2], 0) * inside_z[None, :, None, None]
        flux_y = flux(window_state[:, 2:-2, :, 2:-2], 1) * inside_y[None, None, :, None]
        flux_x = flux(window_state[:, 2:-2, 2:-2, :], 2) * inside_x[None, None, None, :]
        divergence = central(flux_z, 1, CZ) + central(flux_y, 2, NY) + central(flux_x, 3, NX)
        state_block = values + step_size * (-fluid[None] * divergence - sponge * (values - far))
        backward = adjoint(values, central(window_seed[:, :, 2:-2, 2:-2], 1, CZ), 0)
        backward = backward + adjoint(values, central(window_seed[:, 2:-2, :, 2:-2], 2, NY), 1)
        backward = backward + adjoint(values, central(window_seed[:, 2:-2, 2:-2, :], 3, NX), 2)
        gradient = (1.0 - step_size * sponge) * seed_block + backward
        return (state_block, gradient)
    states, gradients = lax.map(block, jnp.arange(NZ // CZ, dtype=jnp.int32))
    state_next = jnp.moveaxis(states, 0, 1).reshape(5, NZ, NY, NX)
    gradient = jnp.moveaxis(gradients, 0, 1).reshape(5, NZ, NY, NX)
    gradient_gain = jnp.sqrt(jnp.sum(gradient * gradient) / (5.0 * NZ * NY * NX) + 1e-06)
    return (state_next, gradient / gradient_gain, gradient_gain)
```

```python
import itertools

import jax
import jax.numpy as jnp
from jax import lax
from jax.experimental import pallas as pl
from jax.experimental.pallas import tpu as pltpu
from jax.sharding import PartitionSpec as P

MESH = pl.DeviceIdType.MESH
f32 = jnp.float32
step_size = 0.25
far_state = (1.0, 0.0, 0.0, 0.5, 0.0)
NC, CZ, NY, NX = 5, 8, 64, 256
LAST = 63
RELAY_A = ((0, 2, 4), (0, 2, 4))
RELAY_B = ((1, 3, 5), (1, 3, 5))
SEND_ORDER = (0, 6, 1, 7, 2, 8, 3, 9, 4, 5)
NR = 3
RELAY_SLOT = 40
W_SEM, F_SEM, R_SEM = 0, 2, 12
STAGES = (
    (("gy", 1, 4), ("gz", 16, 4)),
    (("gz", 4, 4),),
    (("gz", 1, 4),),
)
STAGE_SIZE = (16, 4, 4)
STAGE_START = (0, 16, 20)


def digit(value, stride, size):
    return lax.rem(lax.div(value, stride), size)


def group_of(stage, gz, gy):
    digits = [digit(gy if axis == "gy" else gz, stride, size) for axis, stride, size in stage]
    place = 0
    for (_, _, size), d in zip(stage, digits):
        place = place * size + d
    others = []
    for offset in itertools.product(*[range(size) for _, _, size in stage]):
        if not any(offset):
            continue
        to_z, to_y = gz, gy
        for (axis, stride, size), d, o in zip(stage, digits, offset):
            moved = (lax.rem(d + o, size) - d) * stride
            if axis == "gy":
                to_y = to_y + moved
            else:
                to_z = to_z + moved
        others.append((to_z, to_y))
    return place, others


def shifted_x(cells, lane):
    def at(offset):
        moved = pltpu.roll(cells, (-offset) % NX, 1)
        inside = lane < NX - offset if offset > 0 else lane >= -offset
        return jnp.where(inside, moved, 0.0)

    return at(1) - at(-1), at(2) - at(-2)


def shifted_y(tall):
    def at(offset):
        return tall[8 + offset : 16 + offset]

    return at(1) - at(-1), at(2) - at(-2)


def central(near, wide):
    return near * (8.0 / 12.0) - wide * (1.0 / 12.0)


def velocities(values):
    inverse = 1.0 / values[0]
    return [values[1] * inverse, values[2] * inverse, values[3] * inverse], values[4] * inverse


def sixth_power(density):
    square = density * density
    return square * square * square


def transposed(speeds, ratio, sixth, vector, direction, total):
    along = speeds[direction]
    inner = speeds[0] * vector[1] + speeds[1] * vector[2] + speeds[2] * vector[3] + ratio * vector[4]
    total[0] = total[0] + (sixth * vector[1 + direction] - along * inner)
    for part in range(1, 5):
        total[part] = total[part] + along * vector[part]
    total[1 + direction] = total[1 + direction] + (vector[0] + inner)
    return total


def exchange_kernel(
    state_hbm, seed_hbm, mask_hbm, codes_hbm,
    next_ref, grad_ref, gain_ref,
    st, sd, mk, cd, sponge, w, fz, fy, land, y_out, y_in, parts,
    load_sem, up_sem, down_sem, arrive_sem, forward_sem, y_send, y_arrive, sum_send, sum_arrive,
):
    gz, gy = lax.axis_index("gz"), lax.axis_index("gy")
    spot, z_hi = lax.rem(gz, 16), lax.div(gz, 16)
    has_up, has_down = gz < LAST, gz > 0
    has_right, has_left = gy < 3, gy > 0
    up_corner = (spot == 15) & (z_hi < 3)
    down_corner = (spot == 0) & (z_hi > 0)
    up_relay = ((spot == 12) | (spot == 0)) & (z_hi < 3)
    down_relay = ((spot == 3) | (spot == 15)) & (z_hi > 0)
    first_relay = (spot == 12) | (spot == 3)

    loads = []

    def load(source, target):
        copy = pltpu.make_async_copy(source, target, load_sem.at[len(loads)])
        copy.start()
        loads.append(copy)
        return copy

    ends = (pl.ds(0, 2), pl.ds(CZ - 2, 2))
    middle = pl.ds(2, CZ - 4)
    mask_ends = [load(mask_hbm.at[e], mk.at[e]) for e in ends]
    seed_ends = [load(seed_hbm.at[:, e], sd.at[:, e]) for e in ends]
    mask_middle = load(mask_hbm.at[middle], mk.at[middle])
    seed_middle = load(seed_hbm.at[:, middle], sd.at[:, middle])
    state_all = load(state_hbm, st)
    codes_all = load(codes_hbm, cd)

    barrier = pltpu.get_barrier_semaphore()
    groups = [group_of(stage, gz, gy) for stage in STAGES]
    greeted = 0

    def greet(to_z, to_y):
        pl.semaphore_signal(barrier, inc=1, device_id=(to_z, to_y), device_id_type=MESH)

    for _, others in groups:
        for to_z, to_y in others:
            greet(to_z, to_y)
            greeted = greeted + 1
    for wanted, offsets in (
        (has_up, (1,)),
        (has_down, (-1,)),
        (up_corner, (-3, -15, 4, 16)),
        (down_corner, (3, 15, -4, -16)),
        ((spot == 12) & (z_hi < 3), (3, 4)),
        ((spot == 0) & (z_hi < 3), (15, 16)),
        ((spot == 3) & (z_hi > 0), (-3, -4)),
        ((spot == 15) & (z_hi > 0), (-15, -16)),
    ):

        @pl.when(wanted)
        def _():
            for offset in offsets:
                greet(gz + offset, gy)

        greeted = greeted + jnp.where(wanted, len(offsets), 0)

    def weigh(layer):
        fluid = step_size * mk[layer].astype(f32)
        for c in range(NC):
            w[c, layer + 2, 8 : 8 + NY, :] = fluid * sd[c, layer]

    for copy in mask_ends + seed_ends:
        copy.wait()
    for layer in (0, 1, 6, 7):
        weigh(layer)
    pl.semaphore_wait(barrier, greeted)

    def z_copy(kind, plane, upward):
        component, layer = plane // 2, plane % 2
        source_layer = layer + (CZ - 2 if upward else 0)
        if kind == 0:
            source = w.at[component, source_layer + 2, pl.ds(8, NY)]
        else:
            source = fz.at[component, source_layer + 2]
        side = 0 if upward else 1
        target = gz + 1 if upward else gz - 1
        slot = (side * 2 + kind) * 10 + plane
        arrival = W_SEM + side if kind == 0 else F_SEM + side * NC + component
        corner = up_corner if upward else down_corner
        sign = 1 if upward else -1
        for listed, hop in ((RELAY_A[kind], 3), (RELAY_B[kind], 15)):
            if plane in listed:
                number = kind * NR + listed.index(plane)
                target = jnp.where(corner, gz - sign * hop, target)
                slot = jnp.where(corner, RELAY_SLOT + number, slot)
                arrival = jnp.where(corner, R_SEM + number, arrival)
        return pltpu.make_async_remote_copy(
            src_ref=source,
            dst_ref=land.at[slot],
            send_sem=(up_sem if upward else down_sem).at[0],
            recv_sem=arrive_sem.at[arrival],
            device_id=(target, gy),
            device_id_type=MESH,
        )

    def send_z(kind):
        for plane in SEND_ORDER:

            @pl.when(has_up)
            def _():
                z_copy(kind, plane, True).start()

            @pl.when(has_down)
            def _():
                z_copy(kind, plane, False).start()

    def forward(kind, number):
        index = kind * NR + number
        plane = jnp.where(first_relay, RELAY_A[kind][number], RELAY_B[kind][number])
        component = jnp.where(first_relay, RELAY_A[kind][number] // 2, RELAY_B[kind][number] // 2)
        side = jnp.where(up_relay, 0, 1)
        hop = jnp.where(first_relay, 4, 16)
        target = gz + jnp.where(up_relay, hop, -hop)
        arrival = W_SEM + side if kind == 0 else F_SEM + side * NC + component
        return pltpu.make_async_remote_copy(
            src_ref=land.at[RELAY_SLOT + index],
            dst_ref=land.at[(side * 2 + kind) * 10 + plane],
            send_sem=forward_sem.at[0],
            recv_sem=arrive_sem.at[arrival],
            device_id=(target, gy),
            device_id_type=MESH,
        )

    def relay(kind, number):
        index = kind * NR + number

        def pass_on():
            slot = land.at[RELAY_SLOT + index]
            pltpu.make_async_copy(slot, slot, arrive_sem.at[R_SEM + index]).wait()
            forward(kind, number).start()

        pl.when(up_relay | down_relay)(pass_on)

    def wait_bytes(ref, sem):
        pltpu.make_async_copy(ref, ref, sem).wait()

    send_z(0)

    zero_layer = jnp.zeros((NY, NX), f32)

    def clear(c, carry):
        for layer in (0, 1, CZ + 2, CZ + 3):
            w[c, layer, 8 : 8 + NY, :] = zero_layer
            fz[c, layer] = zero_layer
        return carry

    lax.fori_loop(0, NC, clear, 0)
    mask_middle.wait()
    seed_middle.wait()

    def weigh_more(layer, carry):
        weigh(layer)
        return carry

    lax.fori_loop(2, CZ - 2, weigh_more, 0)

    def y_copy(kind, rightward):
        side = 1 if rightward else 0
        return pltpu.make_async_remote_copy(
            src_ref=y_out.at[side, kind],
            dst_ref=y_in.at[1 - side, kind],
            send_sem=y_send.at[side, kind],
            recv_sem=y_arrive.at[1 - side, kind],
            device_id=(gz, gy + 1 if rightward else gy - 1),
            device_id_type=MESH,
        )

    def send_y(kind, field, first):
        def pack(c, carry):
            for z in range(CZ):
                rows = slice((z % 4) * 2, (z % 4) * 2 + 2)
                y_out[0, kind, c, z // 4, rows, :] = field[c, z + first, 8:10, :]
                y_out[1, kind, c, z // 4, rows, :] = field[c, z + first, 6 + NY : 8 + NY, :]
            return carry

        lax.fori_loop(0, NC, pack, 0)

        @pl.when(has_right)
        def _():
            y_copy(kind, True).start()

        @pl.when(has_left)
        def _():
            y_copy(kind, False).start()

    def take_y(kind, field, first):
        for side, there, at in ((0, has_left, 6), (1, has_right, 8 + NY)):

            @pl.when(there)
            def _():
                y_copy(kind, side == 0).wait_recv()

            @pl.when(jnp.logical_not(there))
            def _():
                y_in[side, kind] = jnp.zeros((NC, 2, 8, NX), f32)

            def unpack(c, carry):
                for z in range(CZ):
                    rows = slice((z % 4) * 2, (z % 4) * 2 + 2)
                    field[c, z + first, at : at + 2, :] = y_in[side, kind, c, z // 4, rows, :]
                return carry

            lax.fori_loop(0, NC, unpack, 0)

    send_y(0, w, 2)

    state_all.wait()
    tiles = NY // 8

    def fluxes(step, carry):
        z, t = lax.div(step, tiles), lax.rem(step, tiles)
        row = pl.multiple_of(t * 8, 8)
        values = [st[c, z, pl.ds(row, 8), :] for c in range(NC)]
        speeds, _ = velocities(values)
        pressure = (sixth_power(values[0]) * values[0] - 1.0) * (1.0 / 7.0)
        for direction, field, first, shift in ((0, fz, 2, 0), (1, fy, 0, 8)):
            rows = pl.ds(pl.multiple_of(row + shift, 8), 8)
            along = speeds[direction]
            field[0, z + first, rows, :] = values[1 + direction]
            for part in range(1, 5):
                flow = values[part] * along
                if part == 1 + direction:
                    flow = flow + pressure
                field[part, z + first, rows, :] = flow
        return carry

    lax.fori_loop(0, CZ * tiles, fluxes, 0, unroll=2)
    send_y(1, fy, 0)
    send_z(1)
    relay(0, 0)

    codes_all.wait()
    line = lax.broadcasted_iota(jnp.int32, (NY, NY), 0)
    column = lax.broadcasted_iota(jnp.int32, (NY, NY), 1)
    for z in range(CZ):
        code = cd[z : z + 1, :]
        strength = jnp.where(code == 1, 0.5, 0.0) + jnp.where(code == 2, 1.0, 0.0) + jnp.where(code == 3, 2.0, 0.0)
        spread = jnp.where(line == column, strength, 0.0)
        sponge[z] = jnp.broadcast_to(step_size * jnp.sum(spread, axis=1, keepdims=True), (NY, NX))

    take_y(0, w, 2)
    take_y(1, fy, 0)

    lane = lax.broadcasted_iota(jnp.int32, (8, NX), 1)

    def cells(step, carry):
        z, t = lax.div(step, tiles), lax.rem(step, tiles)
        row = pl.multiple_of(t * 8, 8)
        rows, tall = pl.ds(row, 8), pl.ds(row, 24)
        shifted_rows = pl.ds(pl.multiple_of(row + 8, 8), 8)
        values = [st[c, z, rows, :] for c in range(NC)]
        fluid = step_size * mk[z, rows, :].astype(f32)
        damping = sponge[z, rows, :]
        speeds, ratio = velocities(values)
        sixth = sixth_power(values[0])
        pressure = (sixth * values[0] - 1.0) * (1.0 / 7.0)
        for c in range(NC):
            flow = values[3] if c == 0 else values[c] * speeds[2]
            if c == 3:
                flow = flow + pressure
            near_x, wide_x = shifted_x(flow, lane)
            near_y, wide_y = shifted_y(fy[c, z, tall, :])
            near = (fz[c, z + 3, rows, :] - fz[c, z + 1, rows, :]) + near_y + near_x
            wide = (fz[c, z + 4, rows, :] - fz[c, z, rows, :]) + wide_y + wide_x
            value = values[c]
            next_ref[c, z, rows, :] = value - fluid * central(near, wide) - damping * (value - far_state[c])
        total = [(1.0 - damping) * sd[c, z, rows, :] for c in range(NC)]
        vector = []
        for c in range(NC):
            near = w[c, z + 3, shifted_rows, :] - w[c, z + 1, shifted_rows, :]
            wide = w[c, z + 4, shifted_rows, :] - w[c, z, shifted_rows, :]
            vector.append(central(near, wide))
        total = transposed(speeds, ratio, sixth, vector, 0, total)
        vector = [central(*shifted_y(w[c, z + 2, tall, :])) for c in range(NC)]
        total = transposed(speeds, ratio, sixth, vector, 1, total)
        vector = [central(*shifted_x(w[c, z + 2, shifted_rows, :], lane)) for c in range(NC)]
        total = transposed(speeds, ratio, sixth, vector, 2, total)
        square = carry
        for c in range(NC):
            grad_ref[c, z, rows, :] = total[c]
            square = square + total[c] * total[c]
        return square

    nothing = jnp.zeros((8, NX), f32)
    lax.fori_loop(0, 2 * tiles, cells, nothing)
    relay(0, 1)
    squares = lax.fori_loop(2 * tiles, 4 * tiles, cells, nothing)
    relay(0, 2)
    squares = lax.fori_loop(4 * tiles, 6 * tiles, cells, squares)
    lax.fori_loop(6 * tiles, 8 * tiles, cells, nothing)
    relay(1, 0)

    for side, there in ((0, has_down), (1, has_up)):
        planes = pl.ds(side * 20, 10)

        @pl.when(there)
        def _():
            wait_bytes(land.at[planes], arrive_sem.at[W_SEM + side])

        @pl.when(jnp.logical_not(there))
        def _():
            land[planes] = jnp.zeros((20 // 2, NY, NX), f32)

    def ends_cells(t, square):
        rows = pl.ds(pl.multiple_of(t * 8, 8), 8)
        for side in range(2):
            outer = [land[side * 20 + 2 * c + side, rows, :] for c in range(NC)]
            inner = [land[side * 20 + 2 * c + 1 - side, rows, :] for c in range(NC)]
            sign = -1.0 if side == 0 else 1.0
            edge, second = (0, 1) if side == 0 else (7, 6)
            cases = (
                (edge, [h1 * (sign * 8.0 / 12.0) - h2 * (sign / 12.0) for h1, h2 in zip(inner, outer)]),
                (second, [h1 * (-sign / 12.0) for h1 in inner]),
            )
            for z, vector in cases:
                values = [st[c, z, rows, :] for c in range(NC)]
                speeds, ratio = velocities(values)
                total = [grad_ref[c, z, rows, :] for c in range(NC)]
                total = transposed(speeds, ratio, sixth_power(values[0]), vector, 0, total)
                for c in range(NC):
                    grad_ref[c, z, rows, :] = total[c]
                    square = square + total[c] * total[c]
        return square

    squares = lax.fori_loop(0, tiles, ends_cells, squares)

    running = squares[:, :128] + squares[:, 128:]
    sends = []
    for number, (place, others) in enumerate(groups):
        size, start = STAGE_SIZE[number], STAGE_START[number]
        parts[start + place] = running
        for to_z, to_y in others:
            pltpu.make_async_remote_copy(
                src_ref=parts.at[start + place],
                dst_ref=parts.at[start + place],
                send_sem=sum_send.at[number],
                recv_sem=sum_arrive.at[number],
                device_id=(to_z, to_y),
                device_id_type=MESH,
            ).start()
        if number == 1:
            relay(1, 1)
            relay(1, 2)
        whole = parts.at[pl.ds(start, size - 1)]
        wait_bytes(whole, sum_arrive.at[number])
        running = parts[start]
        for other in range(1, size):
            running = running + parts[start + other]
        sends.append((whole, sum_send.at[number]))
    count = 1.0 * NC * CZ * NY * NX * 256
    gain_ref[...] = jnp.sqrt(jnp.broadcast_to(jnp.sum(running, keepdims=True), (8, 128)) / count + 1e-06)

    for c in range(NC):
        for side, there in ((0, has_down), (1, has_up)):
            first = side * 20 + 10 + 2 * c

            @pl.when(there)
            def _():
                wait_bytes(land.at[pl.ds(first, 2)], arrive_sem.at[F_SEM + side * NC + c])
                outer, inner = land[first + side], land[first + 1 - side]
                sign = -1.0 if side == 0 else 1.0
                edge, second = (0, 1) if side == 0 else (7, 6)
                cases = (
                    (edge, inner * (sign * 8.0 / 12.0) - outer * (sign / 12.0)),
                    (second, inner * (-sign / 12.0)),
                )
                for z, change in cases:
                    next_ref[c, z] = next_ref[c, z] - step_size * mk[z].astype(f32) * change

    @pl.when(has_up)
    def _():
        wait_bytes(land.at[pl.ds(0, 20)], up_sem.at[0])

    @pl.when(has_down)
    def _():
        wait_bytes(land.at[pl.ds(0, 20)], down_sem.at[0])

    @pl.when(up_relay | down_relay)
    def _():
        wait_bytes(land.at[pl.ds(0, 2 * NR)], forward_sem.at[0])

    for kind in range(2):

        @pl.when(has_right)
        def _():
            y_copy(kind, True).wait_send()

        @pl.when(has_left)
        def _():
            y_copy(kind, False).wait_send()

    for whole, sem in sends:
        wait_bytes(whole, sem)


def finish_kernel(next_vmem, grad_vmem, gain_vmem, next_ref, direction_ref, gain_ref, scaled, sems):
    copies = []
    inverse = jnp.broadcast_to(1.0 / gain_vmem[0:1, 0:1], (NY, NX))
    for c in range(NC):
        copies.append(pltpu.make_async_copy(next_vmem.at[c], next_ref.at[c], sems.at[c]))
        copies[-1].start()
    gain_ref[...] = gain_vmem[0:1, 0:1]
    for c in range(NC):

        def scale(z, carry):
            scaled[c, z] = grad_vmem[c, z] * inverse
            return carry

        lax.fori_loop(0, CZ, scale, 0)
        copies.append(pltpu.make_async_copy(scaled.at[c], direction_ref.at[c], sems.at[NC + c]))
        copies[-1].start()
    for copy in copies:
        copy.wait()


def local(state, adjoint_seed, fluid_mask, boundary_codes):
    block = (NC, CZ, NY, NX)
    inside = [pl.BlockSpec(memory_space=pltpu.VMEM)] * 3
    state_next, gradient, gain = pl.pallas_call(
        exchange_kernel,
        out_shape=[pltpu.VMEM(block, f32), pltpu.VMEM(block, f32), pltpu.VMEM((8, 128), f32)],
        in_specs=[pl.BlockSpec(memory_space=pltpu.HBM)] * 4,
        out_specs=inside,
        scratch_shapes=[
            pltpu.VMEM(block, f32),
            pltpu.VMEM(block, f32),
            pltpu.VMEM((CZ, NY, NX), jnp.int32),
            pltpu.VMEM((CZ, NY), jnp.int32),
            pltpu.VMEM((CZ, NY, NX), f32),
            pltpu.VMEM((NC, CZ + 4, NY + 16, NX), f32),
            pltpu.VMEM((NC, CZ + 4, NY, NX), f32),
            pltpu.VMEM((NC, CZ, NY + 16, NX), f32),
            pltpu.VMEM((RELAY_SLOT + 2 * NR, NY, NX), f32),
            pltpu.VMEM((2, 2, NC, 2, 8, NX), f32),
            pltpu.VMEM((2, 2, NC, 2, 8, NX), f32),
            pltpu.VMEM((24, 8, 128), f32),
            pltpu.SemaphoreType.DMA((8,)),
            pltpu.SemaphoreType.DMA((1,)),
            pltpu.SemaphoreType.DMA((1,)),
            pltpu.SemaphoreType.DMA((R_SEM + 2 * NR,)),
            pltpu.SemaphoreType.DMA((1,)),
            pltpu.SemaphoreType.DMA((2, 2)),
            pltpu.SemaphoreType.DMA((2, 2)),
            pltpu.SemaphoreType.DMA((3,)),
            pltpu.SemaphoreType.DMA((3,)),
        ],
        compiler_params=pltpu.CompilerParams(
            collective_id=0, has_side_effects=True, vmem_limit_bytes=40 * 1024 * 1024
        ),
    )(*[pltpu.with_memory_space_constraint(each, pltpu.HBM) for each in (state, adjoint_seed, fluid_mask, boundary_codes)])
    state_next, direction, gain = pl.pallas_call(
        finish_kernel,
        out_shape=[
            jax.ShapeDtypeStruct(block, f32),
            jax.ShapeDtypeStruct(block, f32),
            jax.ShapeDtypeStruct((1, 1), f32),
        ],
        in_specs=inside,
        out_specs=[
            pl.BlockSpec(memory_space=pl.ANY),
            pl.BlockSpec(memory_space=pl.ANY),
            pl.BlockSpec(memory_space=pltpu.VMEM),
        ],
        scratch_shapes=[pltpu.VMEM(block, f32), pltpu.SemaphoreType.DMA((2 * NC,))],
        compiler_params=pltpu.CompilerParams(vmem_limit_bytes=16 * 1024 * 1024),
    )(state_next, gradient, gain)
    return state_next, direction, gain.reshape(())


def solution(mesh):
    placed = (
        P(None, "gz", "gy", None),
        P(None, "gz", "gy", None),
        P("gz", "gy", None),
        P("gz", "gy"),
    )
    return jax.shard_map(
        local,
        mesh=mesh,
        in_specs=placed,
        out_specs=(P(None, "gz", "gy", None), P(None, "gz", "gy", None), P()),
        check_vma=False,
    )
```

```python
import itertools

import jax
import jax.numpy as jnp
from jax import lax
from jax.experimental import pallas as pl
from jax.experimental.pallas import tpu as pltpu
from jax.sharding import PartitionSpec as P

MESH = pl.DeviceIdType.MESH
f32 = jnp.float32
step_size = 0.25
far_state = (1.0, 0.0, 0.0, 0.5, 0.0)
NC, CZ, NY, NX = 5, 8, 64, 256
LAST = 63
RELAY_A = ((0,2,4,6),(0,2,4,6))
RELAY_B = ((1,3,5,7),(1,3,5,7))
W_FIRST = (8,0,9,1,2,3,4,5,6,7)
W_LATE = ()
F_FIRST = range(8)
F_LATE = (8,9)
PASS_ON = {-1: ((0, 0),), 1: ((0, 1),), 4: ((0, 2),), 7: ((0, 3),), 8: ((1,0),(1,1),(1, 2),), 9: ((1,3),)}
RELAY_START = (0, len(RELAY_A[0]))
RELAYED = len(RELAY_A[0]) + len(RELAY_A[1])
RELAY_SLOT = 40
W_SEM, F_SEM, R_SEM = 0, 2, 12
STAGES = (
    (("gy", 1, 4), ("gz", 16, 4)),
    (("gz", 4, 4), ("gz", 1, 4)),
)
STAGE_SIZE = (16, 16)
STAGE_START = (0, 16)


def digit(value, stride, size):
    return lax.rem(lax.div(value, stride), size)


def group_of(stage, gz, gy):
    digits = [digit(gy if axis == "gy" else gz, stride, size) for axis, stride, size in stage]
    place = 0
    for (_, _, size), d in zip(stage, digits):
        place = place * size + d
    others = []
    for offset in itertools.product(*[range(size) for _, _, size in stage]):
        if not any(offset):
            continue
        to_z, to_y = gz, gy
        for (axis, stride, size), d, o in zip(stage, digits, offset):
            moved = (lax.rem(d + o, size) - d) * stride
            if axis == "gy":
                to_y = to_y + moved
            else:
                to_z = to_z + moved
        others.append((to_z, to_y))
    return place, others


def shifted_x(cells, lane):
    def at(offset):
        moved = pltpu.roll(cells, (-offset) % NX, 1)
        inside = lane < NX - offset if offset > 0 else lane >= -offset
        return jnp.where(inside, moved, 0.0)

    return at(1) - at(-1), at(2) - at(-2)


def shifted_y(tall):
    def at(offset):
        return tall[8 + offset : 16 + offset]

    return at(1) - at(-1), at(2) - at(-2)


def central(near, wide):
    return near * (8.0 / 12.0) - wide * (1.0 / 12.0)


def velocities(values):
    inverse = 1.0 / values[0]
    return [values[1] * inverse, values[2] * inverse, values[3] * inverse], values[4] * inverse


def sixth_power(density):
    square = density * density
    return square * square * square


def transposed(speeds, ratio, sixth, vector, direction, total):
    along = speeds[direction]
    inner = speeds[0] * vector[1] + speeds[1] * vector[2] + speeds[2] * vector[3] + ratio * vector[4]
    total[0] = total[0] + (sixth * vector[1 + direction] - along * inner)
    for part in range(1, 5):
        total[part] = total[part] + along * vector[part]
    total[1 + direction] = total[1 + direction] + (vector[0] + inner)
    return total


def exchange_kernel(
    state_hbm, seed_hbm, mask_hbm, codes_hbm,
    next_ref, grad_ref, gain_ref,
    st, sd, mk, cd, sponge, w, fz, fy, land, y_out, y_in, parts,
    load_sem, up_sem, down_sem, arrive_sem, forward_sem, y_send, y_arrive, sum_send, sum_arrive,
):
    gz, gy = lax.axis_index("gz"), lax.axis_index("gy")
    spot, z_hi = lax.rem(gz, 16), lax.div(gz, 16)
    has_up, has_down = gz < LAST, gz > 0
    has_right, has_left = gy < 3, gy > 0
    up_corner = (spot == 15) & (z_hi < 3)
    down_corner = (spot == 0) & (z_hi > 0)
    up_relay = ((spot == 12) | (spot == 0)) & (z_hi < 3)
    down_relay = ((spot == 3) | (spot == 15)) & (z_hi > 0)
    first_relay = (spot == 12) | (spot == 3)

    loads = []

    def load(source, target):
        copy = pltpu.make_async_copy(source, target, load_sem.at[len(loads)])
        copy.start()
        loads.append(copy)
        return copy

    ends = (pl.ds(0, 2), pl.ds(CZ - 2, 2))
    middle = pl.ds(2, CZ - 4)
    mask_ends = [load(mask_hbm.at[e], mk.at[e]) for e in ends]
    seed_ends = [load(seed_hbm.at[:, e], sd.at[:, e]) for e in ends]
    mask_middle = load(mask_hbm.at[middle], mk.at[middle])
    seed_middle = load(seed_hbm.at[:, middle], sd.at[:, middle])
    state_all = load(state_hbm, st)
    codes_all = load(codes_hbm, cd)

    barrier = pltpu.get_barrier_semaphore()
    groups = [group_of(stage, gz, gy) for stage in STAGES]
    greeted = 0

    def greet(to_z, to_y):
        pl.semaphore_signal(barrier, inc=1, device_id=(to_z, to_y), device_id_type=MESH)

    for _, others in groups:
        for to_z, to_y in others:
            greet(to_z, to_y)
            greeted = greeted + 1
    for wanted, offsets in (
        (has_up, (1,)),
        (has_down, (-1,)),
        (up_corner, (-3, -15, 4, 16)),
        (down_corner, (3, 15, -4, -16)),
        ((spot == 12) & (z_hi < 3), (3, 4)),
        ((spot == 0) & (z_hi < 3), (15, 16)),
        ((spot == 3) & (z_hi > 0), (-3, -4)),
        ((spot == 15) & (z_hi > 0), (-15, -16)),
    ):

        @pl.when(wanted)
        def _():
            for offset in offsets:
                greet(gz + offset, gy)

        greeted = greeted + jnp.where(wanted, len(offsets), 0)

    def weigh(layer):
        fluid = step_size * mk[layer].astype(f32)
        for c in range(NC):
            w[c, layer + 2, 8 : 8 + NY, :] = fluid * sd[c, layer]

    for copy in mask_ends + seed_ends:
        copy.wait()
    for layer in (0, 1, 6, 7):
        weigh(layer)
    pl.semaphore_wait(barrier, greeted)

    def z_copy(kind, plane, upward, at_corner):
        component, layer = plane // 2, plane % 2
        source_layer = layer + (CZ - 2 if upward else 0)
        if kind == 0:
            source = w.at[component, source_layer + 2, pl.ds(8, NY)]
        else:
            source = fz.at[component, source_layer + 2]
        side = 0 if upward else 1
        target = gz + 1 if upward else gz - 1
        slot = (side * 2 + kind) * 10 + plane
        arrival = W_SEM + side if kind == 0 else F_SEM + side * NC + component
        for listed, hop in ((RELAY_A[kind], 3), (RELAY_B[kind], 15)):
            if at_corner and plane in listed:
                number = RELAY_START[kind] + listed.index(plane)
                target = gz - hop if upward else gz + hop
                slot, arrival = RELAY_SLOT + number, R_SEM + number
        return pltpu.make_async_remote_copy(
            src_ref=source,
            dst_ref=land.at[slot],
            send_sem=(up_sem if upward else down_sem).at[0],
            recv_sem=arrive_sem.at[arrival],
            device_id=(target, gy),
            device_id_type=MESH,
        )

    def send_z(kind, order, ways=(True, False)):
        for plane in order:
            for corner, there, upward in ((up_corner, has_up, True), (down_corner, has_down, False)):
                for at_corner in ways:

                    @pl.when(there & (corner if at_corner else jnp.logical_not(corner)))
                    def _():
                        z_copy(kind, plane, upward, at_corner).start()

    def forward(kind, number):
        index = RELAY_START[kind] + number
        plane = jnp.where(first_relay, RELAY_A[kind][number], RELAY_B[kind][number])
        component = jnp.where(first_relay, RELAY_A[kind][number] // 2, RELAY_B[kind][number] // 2)
        side = jnp.where(up_relay, 0, 1)
        hop = jnp.where(first_relay, 4, 16)
        target = gz + jnp.where(up_relay, hop, -hop)
        arrival = W_SEM + side if kind == 0 else F_SEM + side * NC + component
        return pltpu.make_async_remote_copy(
            src_ref=land.at[RELAY_SLOT + index],
            dst_ref=land.at[(side * 2 + kind) * 10 + plane],
            send_sem=forward_sem.at[0],
            recv_sem=arrive_sem.at[arrival],
            device_id=(target, gy),
            device_id_type=MESH,
        )

    def relay(kind, number):
        index = RELAY_START[kind] + number

        def pass_on():
            slot = land.at[RELAY_SLOT + index]
            pltpu.make_async_copy(slot, slot, arrive_sem.at[R_SEM + index]).wait()
            forward(kind, number).start()

        pl.when(up_relay | down_relay)(pass_on)

    def wait_bytes(ref, sem):
        pltpu.make_async_copy(ref, ref, sem).wait()

    send_z(0, range(10), (False,))
    send_z(0, W_FIRST, (True,))

    zero_layer = jnp.zeros((NY, NX), f32)

    def clear(c, carry):
        for layer in (0, 1, CZ + 2, CZ + 3):
            w[c, layer, 8 : 8 + NY, :] = zero_layer
            fz[c, layer] = zero_layer
        return carry

    lax.fori_loop(0, NC, clear, 0)
    mask_middle.wait()
    seed_middle.wait()

    def weigh_more(layer, carry):
        weigh(layer)
        return carry

    lax.fori_loop(2, CZ - 2, weigh_more, 0)

    def y_copy(kind, rightward):
        side = 1 if rightward else 0
        return pltpu.make_async_remote_copy(
            src_ref=y_out.at[side, kind],
            dst_ref=y_in.at[1 - side, kind],
            send_sem=y_send.at[side, kind],
            recv_sem=y_arrive.at[1 - side, kind],
            device_id=(gz, gy + 1 if rightward else gy - 1),
            device_id_type=MESH,
        )

    def send_y(kind, field, first):
        def pack(c, carry):
            for z in range(CZ):
                rows = slice((z % 4) * 2, (z % 4) * 2 + 2)
                y_out[0, kind, c, z // 4, rows, :] = field[c, z + first, 8:10, :]
                y_out[1, kind, c, z // 4, rows, :] = field[c, z + first, 6 + NY : 8 + NY, :]
            return carry

        lax.fori_loop(0, NC, pack, 0)

        @pl.when(has_right)
        def _():
            y_copy(kind, True).start()

        @pl.when(has_left)
        def _():
            y_copy(kind, False).start()

    def take_y(kind, field, first):
        for side, there, at in ((0, has_left, 6), (1, has_right, 8 + NY)):

            @pl.when(there)
            def _():
                y_copy(kind, side == 0).wait_recv()

            @pl.when(jnp.logical_not(there))
            def _():
                y_in[side, kind] = jnp.zeros((NC, 2, 8, NX), f32)

            def unpack(c, carry):
                for z in range(CZ):
                    rows = slice((z % 4) * 2, (z % 4) * 2 + 2)
                    field[c, z + first, at : at + 2, :] = y_in[side, kind, c, z // 4, rows, :]
                return carry

            lax.fori_loop(0, NC, unpack, 0)

    send_y(0, w, 2)

    state_all.wait()
    tiles = NY // 8

    def fluxes(step, carry):
        z, t = lax.div(step, tiles), lax.rem(step, tiles)
        row = pl.multiple_of(t * 8, 8)
        values = [st[c, z, pl.ds(row, 8), :] for c in range(NC)]
        speeds, _ = velocities(values)
        pressure = (sixth_power(values[0]) * values[0] - 1.0) * (1.0 / 7.0)
        for direction, field, first, shift in ((0, fz, 2, 0), (1, fy, 0, 8)):
            rows = pl.ds(pl.multiple_of(row + shift, 8), 8)
            along = speeds[direction]
            field[0, z + first, rows, :] = values[1 + direction]
            for part in range(1, 5):
                flow = values[part] * along
                if part == 1 + direction:
                    flow = flow + pressure
                field[part, z + first, rows, :] = flow
        return carry

    lax.fori_loop(0, CZ * tiles, fluxes, 0, unroll=2)
    send_y(1, fy, 0)
    send_z(0, W_LATE, (True,))
    send_z(1, range(10), (False,))
    send_z(1, F_FIRST, (True,))

    codes_all.wait()
    line = lax.broadcasted_iota(jnp.int32, (NY, NY), 0)
    column = lax.broadcasted_iota(jnp.int32, (NY, NY), 1)
    for z in range(CZ):
        code = cd[z : z + 1, :]
        strength = jnp.where(code == 1, 0.5, 0.0) + jnp.where(code == 2, 1.0, 0.0) + jnp.where(code == 3, 2.0, 0.0)
        spread = jnp.where(line == column, strength, 0.0)
        sponge[z] = jnp.broadcast_to(step_size * jnp.sum(spread, axis=1, keepdims=True), (NY, NX))

    take_y(0, w, 2)
    take_y(1, fy, 0)

    lane = lax.broadcasted_iota(jnp.int32, (8, NX), 1)

    def cells(step, carry):
        z, t = lax.div(step, tiles), lax.rem(step, tiles)
        row = pl.multiple_of(t * 8, 8)
        rows, tall = pl.ds(row, 8), pl.ds(row, 24)
        shifted_rows = pl.ds(pl.multiple_of(row + 8, 8), 8)
        values = [st[c, z, rows, :] for c in range(NC)]
        fluid = step_size * mk[z, rows, :].astype(f32)
        damping = sponge[z, rows, :]
        speeds, ratio = velocities(values)
        sixth = sixth_power(values[0])
        pressure = (sixth * values[0] - 1.0) * (1.0 / 7.0)
        for c in range(NC):
            flow = values[3] if c == 0 else values[c] * speeds[2]
            if c == 3:
                flow = flow + pressure
            near_x, wide_x = shifted_x(flow, lane)
            near_y, wide_y = shifted_y(fy[c, z, tall, :])
            near = (fz[c, z + 3, rows, :] - fz[c, z + 1, rows, :]) + near_y + near_x
            wide = (fz[c, z + 4, rows, :] - fz[c, z, rows, :]) + wide_y + wide_x
            value = values[c]
            next_ref[c, z, rows, :] = value - fluid * central(near, wide) - damping * (value - far_state[c])
        total = [(1.0 - damping) * sd[c, z, rows, :] for c in range(NC)]
        vector = []
        for c in range(NC):
            near = w[c, z + 3, shifted_rows, :] - w[c, z + 1, shifted_rows, :]
            wide = w[c, z + 4, shifted_rows, :] - w[c, z, shifted_rows, :]
            vector.append(central(near, wide))
        total = transposed(speeds, ratio, sixth, vector, 0, total)
        vector = [central(*shifted_y(w[c, z + 2, tall, :])) for c in range(NC)]
        total = transposed(speeds, ratio, sixth, vector, 1, total)
        vector = [central(*shifted_x(w[c, z + 2, shifted_rows, :], lane)) for c in range(NC)]
        total = transposed(speeds, ratio, sixth, vector, 2, total)
        square = carry
        for c in range(NC):
            grad_ref[c, z, rows, :] = total[c]
            square = square + total[c] * total[c]
        return square

    for kind, number in PASS_ON[-1]:
        relay(kind, number)

    def layer_cells(z, carry):
        square = lax.fori_loop(z * tiles, (z + 1) * tiles, cells, carry)

        @pl.when(z == CZ - 1)
        def _():
            send_z(1, F_LATE, (True,))

        for layer, planes in PASS_ON.items():
            if layer < 0 or layer >= CZ:
                continue

            @pl.when(z == layer)
            def _():
                for kind, number in planes:
                    relay(kind, number)

        return jnp.where((z >= 2) & (z < CZ - 2), square, carry)

    squares = lax.fori_loop(0, CZ, layer_cells, jnp.zeros((8, NX), f32))

    for side, there in ((0, has_down), (1, has_up)):
        planes = pl.ds(side * 20, 10)

        @pl.when(there)
        def _():
            wait_bytes(land.at[planes], arrive_sem.at[W_SEM + side])

        @pl.when(jnp.logical_not(there))
        def _():
            land[planes] = jnp.zeros((20 // 2, NY, NX), f32)

    def ends_cells(t, square):
        rows = pl.ds(pl.multiple_of(t * 8, 8), 8)
        for side in range(2):
            outer = [land[side * 20 + 2 * c + side, rows, :] for c in range(NC)]
            inner = [land[side * 20 + 2 * c + 1 - side, rows, :] for c in range(NC)]
            sign = -1.0 if side == 0 else 1.0
            edge, second = (0, 1) if side == 0 else (7, 6)
            cases = (
                (edge, [h1 * (sign * 8.0 / 12.0) - h2 * (sign / 12.0) for h1, h2 in zip(inner, outer)]),
                (second, [h1 * (-sign / 12.0) for h1 in inner]),
            )
            for z, vector in cases:
                values = [st[c, z, rows, :] for c in range(NC)]
                speeds, ratio = velocities(values)
                total = [grad_ref[c, z, rows, :] for c in range(NC)]
                total = transposed(speeds, ratio, sixth_power(values[0]), vector, 0, total)
                for c in range(NC):
                    grad_ref[c, z, rows, :] = total[c]
                    square = square + total[c] * total[c]
        return square

    squares = lax.fori_loop(0, tiles, ends_cells, squares)

    running = squares[:, :128] + squares[:, 128:]
    sends = []
    for number, (place, others) in enumerate(groups):
        size, start = STAGE_SIZE[number], STAGE_START[number]
        parts[start + place] = running
        for to_z, to_y in others:
            pltpu.make_async_remote_copy(
                src_ref=parts.at[start + place],
                dst_ref=parts.at[start + place],
                send_sem=sum_send.at[number],
                recv_sem=sum_arrive.at[number],
                device_id=(to_z, to_y),
                device_id_type=MESH,
            ).start()
        for planes in PASS_ON[CZ + number]:
            relay(*planes)
        whole = parts.at[pl.ds(start, size - 1)]
        wait_bytes(whole, sum_arrive.at[number])
        running = parts[start]
        for other in range(1, size):
            running = running + parts[start + other]
        sends.append((whole, sum_send.at[number]))
    count = 1.0 * NC * CZ * NY * NX * 256
    gain_ref[...] = jnp.sqrt(jnp.broadcast_to(jnp.sum(running, keepdims=True), (8, 128)) / count + 1e-06)

    for c in range(NC):
        for side, there in ((0, has_down), (1, has_up)):
            first = side * 20 + 10 + 2 * c

            @pl.when(there)
            def _():
                wait_bytes(land.at[pl.ds(first, 2)], arrive_sem.at[F_SEM + side * NC + c])
                outer, inner = land[first + side], land[first + 1 - side]
                sign = -1.0 if side == 0 else 1.0
                edge, second = (0, 1) if side == 0 else (7, 6)
                cases = (
                    (edge, inner * (sign * 8.0 / 12.0) - outer * (sign / 12.0)),
                    (second, inner * (-sign / 12.0)),
                )
                for z, change in cases:
                    next_ref[c, z] = next_ref[c, z] - step_size * mk[z].astype(f32) * change

    @pl.when(has_up)
    def _():
        wait_bytes(land.at[pl.ds(0, 20)], up_sem.at[0])

    @pl.when(has_down)
    def _():
        wait_bytes(land.at[pl.ds(0, 20)], down_sem.at[0])

    @pl.when(up_relay | down_relay)
    def _():
        wait_bytes(land.at[pl.ds(0, RELAYED)], forward_sem.at[0])

    for kind in range(2):

        @pl.when(has_right)
        def _():
            y_copy(kind, True).wait_send()

        @pl.when(has_left)
        def _():
            y_copy(kind, False).wait_send()

    for whole, sem in sends:
        wait_bytes(whole, sem)


def finish_kernel(next_vmem, grad_vmem, gain_vmem, next_ref, direction_ref, gain_ref, scaled, sems):
    copies = []
    inverse = jnp.broadcast_to(1.0 / gain_vmem[0:1, 0:1], (NY, NX))
    for c in range(NC):
        copies.append(pltpu.make_async_copy(next_vmem.at[c], next_ref.at[c], sems.at[c]))
        copies[-1].start()
    gain_ref[...] = gain_vmem[0:1, 0:1]
    for c in range(NC):

        def scale(z, carry):
            scaled[c, z] = grad_vmem[c, z] * inverse
            return carry

        lax.fori_loop(0, CZ, scale, 0)
        copies.append(pltpu.make_async_copy(scaled.at[c], direction_ref.at[c], sems.at[NC + c]))
        copies[-1].start()
    for copy in copies:
        copy.wait()


def local(state, adjoint_seed, fluid_mask, boundary_codes):
    block = (NC, CZ, NY, NX)
    inside = [pl.BlockSpec(memory_space=pltpu.VMEM)] * 3
    state_next, gradient, gain = pl.pallas_call(
        exchange_kernel,
        out_shape=[pltpu.VMEM(block, f32), pltpu.VMEM(block, f32), pltpu.VMEM((8, 128), f32)],
        in_specs=[pl.BlockSpec(memory_space=pltpu.HBM)] * 4,
        out_specs=inside,
        scratch_shapes=[
            pltpu.VMEM(block, f32),
            pltpu.VMEM(block, f32),
            pltpu.VMEM((CZ, NY, NX), jnp.int32),
            pltpu.VMEM((CZ, NY), jnp.int32),
            pltpu.VMEM((CZ, NY, NX), f32),
            pltpu.VMEM((NC, CZ + 4, NY + 16, NX), f32),
            pltpu.VMEM((NC, CZ + 4, NY, NX), f32),
            pltpu.VMEM((NC, CZ, NY + 16, NX), f32),
            pltpu.VMEM((RELAY_SLOT + RELAYED, NY, NX), f32),
            pltpu.VMEM((2, 2, NC, 2, 8, NX), f32),
            pltpu.VMEM((2, 2, NC, 2, 8, NX), f32),
            pltpu.VMEM((32, 8, 128), f32),
            pltpu.SemaphoreType.DMA((8,)),
            pltpu.SemaphoreType.DMA((1,)),
            pltpu.SemaphoreType.DMA((1,)),
            pltpu.SemaphoreType.DMA((R_SEM + RELAYED,)),
            pltpu.SemaphoreType.DMA((1,)),
            pltpu.SemaphoreType.DMA((2, 2)),
            pltpu.SemaphoreType.DMA((2, 2)),
            pltpu.SemaphoreType.DMA((2,)),
            pltpu.SemaphoreType.DMA((2,)),
        ],
        compiler_params=pltpu.CompilerParams(
            collective_id=0, has_side_effects=True, vmem_limit_bytes=40 * 1024 * 1024
        ),
    )(*[pltpu.with_memory_space_constraint(each, pltpu.HBM) for each in (state, adjoint_seed, fluid_mask, boundary_codes)])
    state_next, direction, gain = pl.pallas_call(
        finish_kernel,
        out_shape=[
            jax.ShapeDtypeStruct(block, f32),
            jax.ShapeDtypeStruct(block, f32),
            jax.ShapeDtypeStruct((1, 1), f32),
        ],
        in_specs=inside,
        out_specs=[
            pl.BlockSpec(memory_space=pl.ANY),
            pl.BlockSpec(memory_space=pl.ANY),
            pl.BlockSpec(memory_space=pltpu.VMEM),
        ],
        scratch_shapes=[pltpu.VMEM(block, f32), pltpu.SemaphoreType.DMA((2 * NC,))],
        compiler_params=pltpu.CompilerParams(vmem_limit_bytes=16 * 1024 * 1024),
    )(state_next, gradient, gain)
    return state_next, direction, gain.reshape(())


def solution(mesh):
    placed = (
        P(None, "gz", "gy", None),
        P(None, "gz", "gy", None),
        P("gz", "gy", None),
        P("gz", "gy"),
    )
    return jax.shard_map(
        local,
        mesh=mesh,
        in_specs=placed,
        out_specs=(P(None, "gz", "gy", None), P(None, "gz", "gy", None), P()),
        check_vma=False,
    )
```

```python
import itertools

import jax
import jax.numpy as jnp
from jax import lax
from jax.experimental import pallas as pl
from jax.experimental.pallas import tpu as pltpu
from jax.sharding import PartitionSpec as P

MESH = pl.DeviceIdType.MESH
f32 = jnp.float32
step_size = 0.25
far_state = (1.0, 0.0, 0.0, 0.5, 0.0)
NC, CZ, NY, NX = 5, 8, 64, 256
LAST = 63
RELAY_A = ((0,2,4,6),(0,2,4,6))
RELAY_B = ((1,3,5,7),(1,3,5,7))
W_FIRST = (0,1,2,3,4,5,6,7)
W_LATE = (8,9)
F_FIRST = range(8)
F_LATE = (8,9)
PASS_ON = {-1: ((0, 0),), 0: ((0, 1),), 3: ((0, 2),), 6: ((0, 3),), 8: ((1,0),(1,1),(1,2)), 9: ((1,3),)}
RELAY_START = (0, len(RELAY_A[0]))
RELAYED = len(RELAY_A[0]) + len(RELAY_A[1])
RELAY_SLOT = 40
W_SEM, F_SEM, R_SEM = 0, 2, 12
STAGES = (
    (("gy", 1, 4), ("gz", 16, 4)),
    (("gz", 4, 4), ("gz", 1, 4)),
)
STAGE_SIZE = (16, 16)
STAGE_START = (0, 16)


def digit(value, stride, size):
    return lax.rem(lax.div(value, stride), size)


def group_of(stage, gz, gy):
    digits = [digit(gy if axis == "gy" else gz, stride, size) for axis, stride, size in stage]
    place = 0
    for (_, _, size), d in zip(stage, digits):
        place = place * size + d
    others = []
    for offset in itertools.product(*[range(size) for _, _, size in stage]):
        if not any(offset):
            continue
        to_z, to_y = gz, gy
        for (axis, stride, size), d, o in zip(stage, digits, offset):
            moved = (lax.rem(d + o, size) - d) * stride
            if axis == "gy":
                to_y = to_y + moved
            else:
                to_z = to_z + moved
        others.append((to_z, to_y))
    return place, others


def shifted_x(cells, lane):
    def at(offset):
        moved = pltpu.roll(cells, (-offset) % NX, 1)
        inside = lane < NX - offset if offset > 0 else lane >= -offset
        return jnp.where(inside, moved, 0.0)

    return at(1) - at(-1), at(2) - at(-2)


def shifted_y(tall):
    def at(offset):
        return tall[8 + offset : 16 + offset]

    return at(1) - at(-1), at(2) - at(-2)


def central(near, wide):
    return near * (8.0 / 12.0) - wide * (1.0 / 12.0)


def velocities(values):
    inverse = 1.0 / values[0]
    return [values[1] * inverse, values[2] * inverse, values[3] * inverse], values[4] * inverse


def sixth_power(density):
    square = density * density
    return square * square * square


def transposed(speeds, ratio, sixth, vector, direction, total):
    along = speeds[direction]
    inner = speeds[0] * vector[1] + speeds[1] * vector[2] + speeds[2] * vector[3] + ratio * vector[4]
    total[0] = total[0] + (sixth * vector[1 + direction] - along * inner)
    for part in range(1, 5):
        total[part] = total[part] + along * vector[part]
    total[1 + direction] = total[1 + direction] + (vector[0] + inner)
    return total


def exchange_kernel(
    state_hbm, seed_hbm, mask_hbm, codes_hbm,
    next_ref, grad_ref, gain_ref,
    st, sd, mk, cd, sponge, w, fz, fy, land, y_out, y_in, parts,
    load_sem, up_sem, down_sem, arrive_sem, forward_sem, y_send, y_arrive, sum_send, sum_arrive,
):
    gz, gy = lax.axis_index("gz"), lax.axis_index("gy")
    spot, z_hi = lax.rem(gz, 16), lax.div(gz, 16)
    has_up, has_down = gz < LAST, gz > 0
    has_right, has_left = gy < 3, gy > 0
    up_corner = (spot == 15) & (z_hi < 3)
    down_corner = (spot == 0) & (z_hi > 0)
    up_relay = ((spot == 12) | (spot == 0)) & (z_hi < 3)
    down_relay = ((spot == 3) | (spot == 15)) & (z_hi > 0)
    first_relay = (spot == 12) | (spot == 3)

    loads = []

    def load(source, target):
        copy = pltpu.make_async_copy(source, target, load_sem.at[len(loads)])
        copy.start()
        loads.append(copy)
        return copy

    ends = (pl.ds(0, 2), pl.ds(CZ - 2, 2))
    middle = pl.ds(2, CZ - 4)
    mask_ends = [load(mask_hbm.at[e], mk.at[e]) for e in ends]
    seed_ends = [load(seed_hbm.at[:, e], sd.at[:, e]) for e in ends]
    mask_middle = load(mask_hbm.at[middle], mk.at[middle])
    seed_middle = load(seed_hbm.at[:, middle], sd.at[:, middle])
    state_all = load(state_hbm, st)
    codes_all = load(codes_hbm, cd)

    barrier = pltpu.get_barrier_semaphore()
    groups = [group_of(stage, gz, gy) for stage in STAGES]
    greeted = 0

    def greet(to_z, to_y):
        pl.semaphore_signal(barrier, inc=1, device_id=(to_z, to_y), device_id_type=MESH)

    for _, others in groups:
        for to_z, to_y in others:
            greet(to_z, to_y)
            greeted = greeted + 1
    for wanted, offsets in (
        (has_up, (1,)),
        (has_down, (-1,)),
        (up_corner, (-3, -15, 4, 16)),
        (down_corner, (3, 15, -4, -16)),
        ((spot == 12) & (z_hi < 3), (3, 4)),
        ((spot == 0) & (z_hi < 3), (15, 16)),
        ((spot == 3) & (z_hi > 0), (-3, -4)),
        ((spot == 15) & (z_hi > 0), (-15, -16)),
    ):

        @pl.when(wanted)
        def _():
            for offset in offsets:
                greet(gz + offset, gy)

        greeted = greeted + jnp.where(wanted, len(offsets), 0)

    def weigh(layer):
        fluid = step_size * mk[layer].astype(f32)
        for c in range(NC):
            w[c, layer + 2, 8 : 8 + NY, :] = fluid * sd[c, layer]

    for copy in mask_ends + seed_ends:
        copy.wait()
    for layer in (0, 1, 6, 7):
        weigh(layer)
    pl.semaphore_wait(barrier, greeted)

    def z_copy(kind, plane, upward, at_corner):
        component, layer = plane // 2, plane % 2
        source_layer = layer + (CZ - 2 if upward else 0)
        if kind == 0:
            source = w.at[component, source_layer + 2, pl.ds(8, NY)]
        else:
            source = fz.at[component, source_layer + 2]
        side = 0 if upward else 1
        target = gz + 1 if upward else gz - 1
        slot = (side * 2 + kind) * 10 + plane
        arrival = W_SEM + side if kind == 0 else F_SEM + side * NC + component
        for listed, hop in ((RELAY_A[kind], 3), (RELAY_B[kind], 15)):
            if at_corner and plane in listed:
                number = RELAY_START[kind] + listed.index(plane)
                target = gz - hop if upward else gz + hop
                slot, arrival = RELAY_SLOT + number, R_SEM + number
        return pltpu.make_async_remote_copy(
            src_ref=source,
            dst_ref=land.at[slot],
            send_sem=(up_sem if upward else down_sem).at[0],
            recv_sem=arrive_sem.at[arrival],
            device_id=(target, gy),
            device_id_type=MESH,
        )

    def send_z(kind, order, ways=(True, False)):
        for plane in order:
            for corner, there, upward in ((up_corner, has_up, True), (down_corner, has_down, False)):
                for at_corner in ways:

                    @pl.when(there & (corner if at_corner else jnp.logical_not(corner)))
                    def _():
                        z_copy(kind, plane, upward, at_corner).start()

    def forward(kind, number):
        index = RELAY_START[kind] + number
        plane = jnp.where(first_relay, RELAY_A[kind][number], RELAY_B[kind][number])
        component = jnp.where(first_relay, RELAY_A[kind][number] // 2, RELAY_B[kind][number] // 2)
        side = jnp.where(up_relay, 0, 1)
        hop = jnp.where(first_relay, 4, 16)
        target = gz + jnp.where(up_relay, hop, -hop)
        arrival = W_SEM + side if kind == 0 else F_SEM + side * NC + component
        return pltpu.make_async_remote_copy(
            src_ref=land.at[RELAY_SLOT + index],
            dst_ref=land.at[(side * 2 + kind) * 10 + plane],
            send_sem=forward_sem.at[0],
            recv_sem=arrive_sem.at[arrival],
            device_id=(target, gy),
            device_id_type=MESH,
        )

    def relay(kind, number):
        index = RELAY_START[kind] + number

        def pass_on():
            slot = land.at[RELAY_SLOT + index]
            pltpu.make_async_copy(slot, slot, arrive_sem.at[R_SEM + index]).wait()
            forward(kind, number).start()

        pl.when(up_relay | down_relay)(pass_on)

    def wait_bytes(ref, sem):
        pltpu.make_async_copy(ref, ref, sem).wait()

    send_z(0, range(10), (False,))
    send_z(0, W_FIRST, (True,))

    zero_layer = jnp.zeros((NY, NX), f32)

    def clear(c, carry):
        for layer in (0, 1, CZ + 2, CZ + 3):
            w[c, layer, 8 : 8 + NY, :] = zero_layer
            fz[c, layer] = zero_layer
        return carry

    lax.fori_loop(0, NC, clear, 0)
    mask_middle.wait()
    seed_middle.wait()

    def weigh_more(layer, carry):
        weigh(layer)
        return carry

    lax.fori_loop(2, CZ - 2, weigh_more, 0)

    def y_copy(kind, rightward):
        side = 1 if rightward else 0
        return pltpu.make_async_remote_copy(
            src_ref=y_out.at[side, kind],
            dst_ref=y_in.at[1 - side, kind],
            send_sem=y_send.at[side, kind],
            recv_sem=y_arrive.at[1 - side, kind],
            device_id=(gz, gy + 1 if rightward else gy - 1),
            device_id_type=MESH,
        )

    def send_y(kind, field, first):
        def pack(c, carry):
            for z in range(CZ):
                rows = slice((z % 4) * 2, (z % 4) * 2 + 2)
                y_out[0, kind, c, z // 4, rows, :] = field[c, z + first, 8:10, :]
                y_out[1, kind, c, z // 4, rows, :] = field[c, z + first, 6 + NY : 8 + NY, :]
            return carry

        lax.fori_loop(0, NC, pack, 0)

        @pl.when(has_right)
        def _():
            y_copy(kind, True).start()

        @pl.when(has_left)
        def _():
            y_copy(kind, False).start()

    def take_y(kind, field, first):
        for side, there, at in ((0, has_left, 6), (1, has_right, 8 + NY)):

            @pl.when(there)
            def _():
                y_copy(kind, side == 0).wait_recv()

            @pl.when(jnp.logical_not(there))
            def _():
                y_in[side, kind] = jnp.zeros((NC, 2, 8, NX), f32)

            def unpack(c, carry):
                for z in range(CZ):
                    rows = slice((z % 4) * 2, (z % 4) * 2 + 2)
                    field[c, z + first, at : at + 2, :] = y_in[side, kind, c, z // 4, rows, :]
                return carry

            lax.fori_loop(0, NC, unpack, 0)

    send_y(0, w, 2)

    state_all.wait()
    tiles = NY // 8

    def fluxes(step, carry):
        z, t = lax.div(step, tiles), lax.rem(step, tiles)
        row = pl.multiple_of(t * 8, 8)
        values = [st[c, z, pl.ds(row, 8), :] for c in range(NC)]
        speeds, _ = velocities(values)
        pressure = (sixth_power(values[0]) * values[0] - 1.0) * (1.0 / 7.0)
        for direction, field, first, shift in ((0, fz, 2, 0), (1, fy, 0, 8)):
            rows = pl.ds(pl.multiple_of(row + shift, 8), 8)
            along = speeds[direction]
            field[0, z + first, rows, :] = values[1 + direction]
            for part in range(1, 5):
                flow = values[part] * along
                if part == 1 + direction:
                    flow = flow + pressure
                field[part, z + first, rows, :] = flow
        return carry

    lax.fori_loop(0, CZ * tiles, fluxes, 0, unroll=2)
    send_y(1, fy, 0)
    send_z(0, W_LATE, (True,))
    send_z(1, range(10), (False,))
    send_z(1, F_FIRST, (True,))

    codes_all.wait()
    line = lax.broadcasted_iota(jnp.int32, (NY, NY), 0)
    column = lax.broadcasted_iota(jnp.int32, (NY, NY), 1)
    for z in range(CZ):
        code = cd[z : z + 1, :]
        strength = jnp.where(code == 1, 0.5, 0.0) + jnp.where(code == 2, 1.0, 0.0) + jnp.where(code == 3, 2.0, 0.0)
        spread = jnp.where(line == column, strength, 0.0)
        sponge[z] = jnp.broadcast_to(step_size * jnp.sum(spread, axis=1, keepdims=True), (NY, NX))

    take_y(0, w, 2)
    take_y(1, fy, 0)

    lane = lax.broadcasted_iota(jnp.int32, (8, NX), 1)

    def cells(step, carry):
        z, t = lax.div(step, tiles), lax.rem(step, tiles)
        row = pl.multiple_of(t * 8, 8)
        rows, tall = pl.ds(row, 8), pl.ds(row, 24)
        shifted_rows = pl.ds(pl.multiple_of(row + 8, 8), 8)
        values = [st[c, z, rows, :] for c in range(NC)]
        fluid = step_size * mk[z, rows, :].astype(f32)
        damping = sponge[z, rows, :]
        speeds, ratio = velocities(values)
        sixth = sixth_power(values[0])
        pressure = (sixth * values[0] - 1.0) * (1.0 / 7.0)
        for c in range(NC):
            flow = values[3] if c == 0 else values[c] * speeds[2]
            if c == 3:
                flow = flow + pressure
            near_x, wide_x = shifted_x(flow, lane)
            near_y, wide_y = shifted_y(fy[c, z, tall, :])
            near = (fz[c, z + 3, rows, :] - fz[c, z + 1, rows, :]) + near_y + near_x
            wide = (fz[c, z + 4, rows, :] - fz[c, z, rows, :]) + wide_y + wide_x
            value = values[c]
            next_ref[c, z, rows, :] = value - fluid * central(near, wide) - damping * (value - far_state[c])
        total = [(1.0 - damping) * sd[c, z, rows, :] for c in range(NC)]
        vector = []
        for c in range(NC):
            near = w[c, z + 3, shifted_rows, :] - w[c, z + 1, shifted_rows, :]
            wide = w[c, z + 4, shifted_rows, :] - w[c, z, shifted_rows, :]
            vector.append(central(near, wide))
        total = transposed(speeds, ratio, sixth, vector, 0, total)
        vector = [central(*shifted_y(w[c, z + 2, tall, :])) for c in range(NC)]
        total = transposed(speeds, ratio, sixth, vector, 1, total)
        vector = [central(*shifted_x(w[c, z + 2, shifted_rows, :], lane)) for c in range(NC)]
        total = transposed(speeds, ratio, sixth, vector, 2, total)
        square = carry
        for c in range(NC):
            grad_ref[c, z, rows, :] = total[c]
            square = square + total[c] * total[c]
        return square

    for kind, number in PASS_ON[-1]:
        relay(kind, number)

    def layer_cells(z, carry):
        square = lax.fori_loop(z * tiles, (z + 1) * tiles, cells, carry)

        @pl.when(z == CZ - 1)
        def _():
            send_z(1, F_LATE, (True,))

        for layer, planes in PASS_ON.items():
            if layer < 0 or layer >= CZ:
                continue

            @pl.when(z == layer)
            def _():
                for kind, number in planes:
                    relay(kind, number)

        return jnp.where((z >= 2) & (z < CZ - 2), square, carry)

    squares = lax.fori_loop(0, CZ, layer_cells, jnp.zeros((8, NX), f32))

    for side, there in ((0, has_down), (1, has_up)):
        planes = pl.ds(side * 20, 10)

        @pl.when(there)
        def _():
            wait_bytes(land.at[planes], arrive_sem.at[W_SEM + side])

        @pl.when(jnp.logical_not(there))
        def _():
            land[planes] = jnp.zeros((20 // 2, NY, NX), f32)

    def ends_cells(t, square):
        rows = pl.ds(pl.multiple_of(t * 8, 8), 8)
        for side in range(2):
            outer = [land[side * 20 + 2 * c + side, rows, :] for c in range(NC)]
            inner = [land[side * 20 + 2 * c + 1 - side, rows, :] for c in range(NC)]
            sign = -1.0 if side == 0 else 1.0
            edge, second = (0, 1) if side == 0 else (7, 6)
            cases = (
                (edge, [h1 * (sign * 8.0 / 12.0) - h2 * (sign / 12.0) for h1, h2 in zip(inner, outer)]),
                (second, [h1 * (-sign / 12.0) for h1 in inner]),
            )
            for z, vector in cases:
                values = [st[c, z, rows, :] for c in range(NC)]
                speeds, ratio = velocities(values)
                total = [grad_ref[c, z, rows, :] for c in range(NC)]
                total = transposed(speeds, ratio, sixth_power(values[0]), vector, 0, total)
                for c in range(NC):
                    grad_ref[c, z, rows, :] = total[c]
                    square = square + total[c] * total[c]
        return square

    squares = lax.fori_loop(0, tiles, ends_cells, squares)

    running = squares[:, :128] + squares[:, 128:]
    sends = []
    for number, (place, others) in enumerate(groups):
        size, start = STAGE_SIZE[number], STAGE_START[number]
        parts[start + place] = running
        for to_z, to_y in others:
            pltpu.make_async_remote_copy(
                src_ref=parts.at[start + place],
                dst_ref=parts.at[start + place],
                send_sem=sum_send.at[number],
                recv_sem=sum_arrive.at[number],
                device_id=(to_z, to_y),
                device_id_type=MESH,
            ).start()
        for planes in PASS_ON[CZ + number]:
            relay(*planes)
        whole = parts.at[pl.ds(start, size - 1)]
        wait_bytes(whole, sum_arrive.at[number])
        running = parts[start]
        for other in range(1, size):
            running = running + parts[start + other]
        sends.append((whole, sum_send.at[number]))
    count = 1.0 * NC * CZ * NY * NX * 256
    gain_ref[...] = jnp.sqrt(jnp.broadcast_to(jnp.sum(running, keepdims=True), (8, 128)) / count + 1e-06)

    for c in range(NC):
        for side, there in ((0, has_down), (1, has_up)):
            first = side * 20 + 10 + 2 * c

            @pl.when(there)
            def _():
                wait_bytes(land.at[pl.ds(first, 2)], arrive_sem.at[F_SEM + side * NC + c])
                outer, inner = land[first + side], land[first + 1 - side]
                sign = -1.0 if side == 0 else 1.0
                edge, second = (0, 1) if side == 0 else (7, 6)
                cases = (
                    (edge, inner * (sign * 8.0 / 12.0) - outer * (sign / 12.0)),
                    (second, inner * (-sign / 12.0)),
                )
                for z, change in cases:
                    next_ref[c, z] = next_ref[c, z] - step_size * mk[z].astype(f32) * change

    @pl.when(has_up)
    def _():
        wait_bytes(land.at[pl.ds(0, 20)], up_sem.at[0])

    @pl.when(has_down)
    def _():
        wait_bytes(land.at[pl.ds(0, 20)], down_sem.at[0])

    @pl.when(up_relay | down_relay)
    def _():
        wait_bytes(land.at[pl.ds(0, RELAYED)], forward_sem.at[0])

    for kind in range(2):

        @pl.when(has_right)
        def _():
            y_copy(kind, True).wait_send()

        @pl.when(has_left)
        def _():
            y_copy(kind, False).wait_send()

    for whole, sem in sends:
        wait_bytes(whole, sem)


def finish_kernel(next_vmem, grad_vmem, gain_vmem, next_ref, direction_ref, gain_ref, scaled, sems):
    copies = []
    inverse = jnp.broadcast_to(1.0 / gain_vmem[0:1, 0:1], (NY, NX))
    for c in range(NC):
        copies.append(pltpu.make_async_copy(next_vmem.at[c], next_ref.at[c], sems.at[c]))
        copies[-1].start()
    gain_ref[...] = gain_vmem[0:1, 0:1]
    for c in range(NC):

        def scale(z, carry):
            scaled[c, z] = grad_vmem[c, z] * inverse
            return carry

        lax.fori_loop(0, CZ, scale, 0)
        copies.append(pltpu.make_async_copy(scaled.at[c], direction_ref.at[c], sems.at[NC + c]))
        copies[-1].start()
    for copy in copies:
        copy.wait()


def local(state, adjoint_seed, fluid_mask, boundary_codes):
    block = (NC, CZ, NY, NX)
    inside = [pl.BlockSpec(memory_space=pltpu.VMEM)] * 3
    state_next, gradient, gain = pl.pallas_call(
        exchange_kernel,
        out_shape=[pltpu.VMEM(block, f32), pltpu.VMEM(block, f32), pltpu.VMEM((8, 128), f32)],
        in_specs=[pl.BlockSpec(memory_space=pltpu.HBM)] * 4,
        out_specs=inside,
        scratch_shapes=[
            pltpu.VMEM(block, f32),
            pltpu.VMEM(block, f32),
            pltpu.VMEM((CZ, NY, NX), jnp.int32),
            pltpu.VMEM((CZ, NY), jnp.int32),
            pltpu.VMEM((CZ, NY, NX), f32),
            pltpu.VMEM((NC, CZ + 4, NY + 16, NX), f32),
            pltpu.VMEM((NC, CZ + 4, NY, NX), f32),
            pltpu.VMEM((NC, CZ, NY + 16, NX), f32),
            pltpu.VMEM((RELAY_SLOT + RELAYED, NY, NX), f32),
            pltpu.VMEM((2, 2, NC, 2, 8, NX), f32),
            pltpu.VMEM((2, 2, NC, 2, 8, NX), f32),
            pltpu.VMEM((32, 8, 128), f32),
            pltpu.SemaphoreType.DMA((8,)),
            pltpu.SemaphoreType.DMA((1,)),
            pltpu.SemaphoreType.DMA((1,)),
            pltpu.SemaphoreType.DMA((R_SEM + RELAYED,)),
            pltpu.SemaphoreType.DMA((1,)),
            pltpu.SemaphoreType.DMA((2, 2)),
            pltpu.SemaphoreType.DMA((2, 2)),
            pltpu.SemaphoreType.DMA((2,)),
            pltpu.SemaphoreType.DMA((2,)),
        ],
        compiler_params=pltpu.CompilerParams(
            collective_id=0, has_side_effects=True, vmem_limit_bytes=40 * 1024 * 1024
        ),
    )(*[pltpu.with_memory_space_constraint(each, pltpu.HBM) for each in (state, adjoint_seed, fluid_mask, boundary_codes)])
    state_next, direction, gain = pl.pallas_call(
        finish_kernel,
        out_shape=[
            jax.ShapeDtypeStruct(block, f32),
            jax.ShapeDtypeStruct(block, f32),
            jax.ShapeDtypeStruct((1, 1), f32),
        ],
        in_specs=inside,
        out_specs=[
            pl.BlockSpec(memory_space=pl.ANY),
            pl.BlockSpec(memory_space=pl.ANY),
            pl.BlockSpec(memory_space=pltpu.VMEM),
        ],
        scratch_shapes=[pltpu.VMEM(block, f32), pltpu.SemaphoreType.DMA((2 * NC,))],
        compiler_params=pltpu.CompilerParams(vmem_limit_bytes=16 * 1024 * 1024),
    )(state_next, gradient, gain)
    return state_next, direction, gain.reshape(())


def solution(mesh):
    placed = (
        P(None, "gz", "gy", None),
        P(None, "gz", "gy", None),
        P("gz", "gy", None),
        P("gz", "gy"),
    )
    return jax.shard_map(
        local,
        mesh=mesh,
        in_specs=placed,
        out_specs=(P(None, "gz", "gy", None), P(None, "gz", "gy", None), P()),
        check_vma=False,
    )
```

```python
import itertools

import jax
import jax.numpy as jnp
from jax import lax
from jax.experimental import pallas as pl
from jax.experimental.pallas import tpu as pltpu
from jax.sharding import PartitionSpec as P

MESH = pl.DeviceIdType.MESH
f32 = jnp.float32
step_size = 0.25
far_state = (1.0, 0.0, 0.0, 0.5, 0.0)
NC, CZ, NY, NX = 5, 8, 64, 256
LAST = 63
RELAY_A = ((0,2,4,6),(0,2,4,6))
RELAY_B = ((1,3,5,7),(1,3,5,7))
W_FIRST = (0,1,2,3,4,5,6,7)
W_LATE = (8,9)
F_FIRST = range(8)
F_LATE = (8,9)
PASS_ON = {-1: ((0, 0),), 0: ((0, 1),), 3: ((0, 2),), 6: ((0, 3),), 8: ((1,0),(1,1),(1,2)), 9: ((1,3),)}
RELAY_START = (0, len(RELAY_A[0]))
RELAYED = len(RELAY_A[0]) + len(RELAY_A[1])
RELAY_SLOT = 40
W_SEM, F_SEM, R_SEM = 0, 2, 12
STAGES = (
    (("gy", 1, 4), ("gz", 16, 4)),
    (("gz", 4, 4), ("gz", 1, 4)),
)
STAGE_SIZE = (16, 16)
STAGE_START = (0, 16)


def digit(value, stride, size):
    return lax.rem(lax.div(value, stride), size)


def group_of(stage, gz, gy):
    digits = [digit(gy if axis == "gy" else gz, stride, size) for axis, stride, size in stage]
    place = 0
    for (_, _, size), d in zip(stage, digits):
        place = place * size + d
    others = []
    for offset in itertools.product(*[range(size) for _, _, size in stage]):
        if not any(offset):
            continue
        to_z, to_y = gz, gy
        for (axis, stride, size), d, o in zip(stage, digits, offset):
            moved = (lax.rem(d + o, size) - d) * stride
            if axis == "gy":
                to_y = to_y + moved
            else:
                to_z = to_z + moved
        others.append((to_z, to_y))
    return place, others


def shifted_x(cells, lane):
    def at(offset):
        moved = pltpu.roll(cells, (-offset) % NX, 1)
        inside = lane < NX - offset if offset > 0 else lane >= -offset
        return jnp.where(inside, moved, 0.0)

    return at(1) - at(-1), at(2) - at(-2)


def shifted_y(tall):
    def at(offset):
        return tall[8 + offset : 16 + offset]

    return at(1) - at(-1), at(2) - at(-2)


def central(near, wide):
    return near * (8.0 / 12.0) - wide * (1.0 / 12.0)


def velocities(values):
    inverse = 1.0 / values[0]
    return [values[1] * inverse, values[2] * inverse, values[3] * inverse], values[4] * inverse


def sixth_power(density):
    square = density * density
    return square * square * square


def transposed(speeds, ratio, sixth, vector, direction, total):
    along = speeds[direction]
    inner = speeds[0] * vector[1] + speeds[1] * vector[2] + speeds[2] * vector[3] + ratio * vector[4]
    total[0] = total[0] + (sixth * vector[1 + direction] - along * inner)
    for part in range(1, 5):
        total[part] = total[part] + along * vector[part]
    total[1 + direction] = total[1 + direction] + (vector[0] + inner)
    return total


def exchange_kernel(
    state_hbm, seed_hbm, mask_hbm, codes_hbm,
    next_ref, grad_ref, gain_ref,
    st, sd, mk, cd, sponge, w, fz, fy, land, y_out, y_in, parts,
    load_sem, up_sem, down_sem, arrive_sem, forward_sem, y_send, y_arrive, sum_send, sum_arrive,
):
    gz, gy = lax.axis_index("gz"), lax.axis_index("gy")
    spot, z_hi = lax.rem(gz, 16), lax.div(gz, 16)
    has_up, has_down = gz < LAST, gz > 0
    has_right, has_left = gy < 3, gy > 0
    up_corner = (spot == 15) & (z_hi < 3)
    down_corner = (spot == 0) & (z_hi > 0)
    up_relay = ((spot == 12) | (spot == 0)) & (z_hi < 3)
    down_relay = ((spot == 3) | (spot == 15)) & (z_hi > 0)
    first_relay = (spot == 12) | (spot == 3)

    loads = []

    def load(source, target):
        copy = pltpu.make_async_copy(source, target, load_sem.at[len(loads)])
        copy.start()
        loads.append(copy)
        return copy

    ends = (pl.ds(0, 2), pl.ds(CZ - 2, 2))
    middle = pl.ds(2, CZ - 4)
    mask_ends = [load(mask_hbm.at[e], mk.at[e]) for e in ends]
    seed_ends = [load(seed_hbm.at[:, e], sd.at[:, e]) for e in ends]
    mask_middle = load(mask_hbm.at[middle], mk.at[middle])
    seed_middle = load(seed_hbm.at[:, middle], sd.at[:, middle])
    state_all = load(state_hbm, st)
    codes_all = load(codes_hbm, cd)

    barrier = pltpu.get_barrier_semaphore()
    groups = [group_of(stage, gz, gy) for stage in STAGES]
    greeted = 0

    def greet(to_z, to_y):
        pl.semaphore_signal(barrier, inc=1, device_id=(to_z, to_y), device_id_type=MESH)

    for _, others in groups:
        for to_z, to_y in others:
            greet(to_z, to_y)
            greeted = greeted + 1
    for wanted, offsets in (
        (has_up, (1,)),
        (has_down, (-1,)),
        (up_corner, (-3, -15, 4, 16)),
        (down_corner, (3, 15, -4, -16)),
        ((spot == 12) & (z_hi < 3), (3, 4)),
        ((spot == 0) & (z_hi < 3), (15, 16)),
        ((spot == 3) & (z_hi > 0), (-3, -4)),
        ((spot == 15) & (z_hi > 0), (-15, -16)),
    ):

        @pl.when(wanted)
        def _():
            for offset in offsets:
                greet(gz + offset, gy)

        greeted = greeted + jnp.where(wanted, len(offsets), 0)

    def weigh(layer):
        fluid = step_size * mk[layer].astype(f32)
        for c in range(NC):
            w[c, layer + 2, 8 : 8 + NY, :] = fluid * sd[c, layer]

    for copy in mask_ends + seed_ends:
        copy.wait()
    for layer in (0, 1, 6, 7):
        weigh(layer)
    pl.semaphore_wait(barrier, greeted)

    def z_copy(kind, plane, upward, at_corner):
        component, layer = plane // 2, plane % 2
        source_layer = layer + (CZ - 2 if upward else 0)
        if kind == 0:
            source = w.at[component, source_layer + 2, pl.ds(8, NY)]
        else:
            source = fz.at[component, source_layer + 2]
        side = 0 if upward else 1
        target = gz + 1 if upward else gz - 1
        slot = (side * 2 + kind) * 10 + plane
        arrival = W_SEM + side if kind == 0 else F_SEM + side * NC + component
        for listed, hop in ((RELAY_A[kind], 3), (RELAY_B[kind], 15)):
            if at_corner and plane in listed:
                number = RELAY_START[kind] + listed.index(plane)
                target = gz - hop if upward else gz + hop
                slot, arrival = RELAY_SLOT + number, R_SEM + number
        return pltpu.make_async_remote_copy(
            src_ref=source,
            dst_ref=land.at[slot],
            send_sem=(up_sem if upward else down_sem).at[0],
            recv_sem=arrive_sem.at[arrival],
            device_id=(target, gy),
            device_id_type=MESH,
        )

    def send_z(kind, order, ways=(True, False)):
        for plane in order:
            for corner, there, upward in ((up_corner, has_up, True), (down_corner, has_down, False)):
                for at_corner in ways:

                    @pl.when(there & (corner if at_corner else jnp.logical_not(corner)))
                    def _():
                        z_copy(kind, plane, upward, at_corner).start()

    def forward(kind, number):
        index = RELAY_START[kind] + number
        plane = jnp.where(first_relay, RELAY_A[kind][number], RELAY_B[kind][number])
        component = jnp.where(first_relay, RELAY_A[kind][number] // 2, RELAY_B[kind][number] // 2)
        side = jnp.where(up_relay, 0, 1)
        hop = jnp.where(first_relay, 4, 16)
        target = gz + jnp.where(up_relay, hop, -hop)
        arrival = W_SEM + side if kind == 0 else F_SEM + side * NC + component
        return pltpu.make_async_remote_copy(
            src_ref=land.at[RELAY_SLOT + index],
            dst_ref=land.at[(side * 2 + kind) * 10 + plane],
            send_sem=forward_sem.at[0],
            recv_sem=arrive_sem.at[arrival],
            device_id=(target, gy),
            device_id_type=MESH,
        )

    def relay(kind, number):
        index = RELAY_START[kind] + number

        def pass_on():
            slot = land.at[RELAY_SLOT + index]
            pltpu.make_async_copy(slot, slot, arrive_sem.at[R_SEM + index]).wait()
            forward(kind, number).start()

        pl.when(up_relay | down_relay)(pass_on)

    def wait_bytes(ref, sem):
        pltpu.make_async_copy(ref, ref, sem).wait()

    send_z(0, range(10), (False,))
    send_z(0, W_FIRST, (True,))

    zero_layer = jnp.zeros((NY, NX), f32)

    def clear(c, carry):
        for layer in (0, 1, CZ + 2, CZ + 3):
            w[c, layer, 8 : 8 + NY, :] = zero_layer
            fz[c, layer] = zero_layer
        return carry

    lax.fori_loop(0, NC, clear, 0)
    mask_middle.wait()
    seed_middle.wait()

    def weigh_more(layer, carry):
        weigh(layer)
        return carry

    lax.fori_loop(2, CZ - 2, weigh_more, 0)

    def y_copy(kind, rightward):
        side = 1 if rightward else 0
        return pltpu.make_async_remote_copy(
            src_ref=y_out.at[side, kind],
            dst_ref=y_in.at[1 - side, kind],
            send_sem=y_send.at[side, kind],
            recv_sem=y_arrive.at[1 - side, kind],
            device_id=(gz, gy + 1 if rightward else gy - 1),
            device_id_type=MESH,
        )

    def send_y(kind, field, first):
        def pack(c, carry):
            for z in range(CZ):
                rows = slice((z % 4) * 2, (z % 4) * 2 + 2)
                y_out[0, kind, c, z // 4, rows, :] = field[c, z + first, 8:10, :]
                y_out[1, kind, c, z // 4, rows, :] = field[c, z + first, 6 + NY : 8 + NY, :]
            return carry

        lax.fori_loop(0, NC, pack, 0)

        @pl.when(has_right)
        def _():
            y_copy(kind, True).start()

        @pl.when(has_left)
        def _():
            y_copy(kind, False).start()

    def take_y(kind, field, first):
        for side, there, at in ((0, has_left, 6), (1, has_right, 8 + NY)):

            @pl.when(there)
            def _():
                y_copy(kind, side == 0).wait_recv()

            @pl.when(jnp.logical_not(there))
            def _():
                y_in[side, kind] = jnp.zeros((NC, 2, 8, NX), f32)

            def unpack(c, carry):
                for z in range(CZ):
                    rows = slice((z % 4) * 2, (z % 4) * 2 + 2)
                    field[c, z + first, at : at + 2, :] = y_in[side, kind, c, z // 4, rows, :]
                return carry

            lax.fori_loop(0, NC, unpack, 0)

    send_y(0, w, 2)

    state_all.wait()
    tiles = NY // 8

    def fluxes(step, carry):
        z, t = lax.div(step, tiles), lax.rem(step, tiles)
        row = pl.multiple_of(t * 8, 8)
        values = [st[c, z, pl.ds(row, 8), :] for c in range(NC)]
        speeds, _ = velocities(values)
        pressure = (sixth_power(values[0]) * values[0] - 1.0) * (1.0 / 7.0)
        for direction, field, first, shift in ((0, fz, 2, 0), (1, fy, 0, 8)):
            rows = pl.ds(pl.multiple_of(row + shift, 8), 8)
            along = speeds[direction]
            field[0, z + first, rows, :] = values[1 + direction]
            for part in range(1, 5):
                flow = values[part] * along
                if part == 1 + direction:
                    flow = flow + pressure
                field[part, z + first, rows, :] = flow
        return carry

    lax.fori_loop(0, CZ * tiles, fluxes, 0, unroll=2)
    send_y(1, fy, 0)
    send_z(0, W_LATE, (True,))
    send_z(1, range(10), (False,))
    send_z(1, F_FIRST, (True,))

    codes_all.wait()
    line = lax.broadcasted_iota(jnp.int32, (NY, NY), 0)
    column = lax.broadcasted_iota(jnp.int32, (NY, NY), 1)
    for z in range(CZ):
        code = cd[z : z + 1, :]
        strength = jnp.where(code == 1, 0.5, 0.0) + jnp.where(code == 2, 1.0, 0.0) + jnp.where(code == 3, 2.0, 0.0)
        spread = jnp.where(line == column, strength, 0.0)
        sponge[z] = jnp.broadcast_to(step_size * jnp.sum(spread, axis=1, keepdims=True), (NY, NX))

    take_y(0, w, 2)
    take_y(1, fy, 0)

    lane = lax.broadcasted_iota(jnp.int32, (8, NX), 1)

    def cells(step, carry):
        z, t = lax.div(step, tiles), lax.rem(step, tiles)
        row = pl.multiple_of(t * 8, 8)
        rows, tall = pl.ds(row, 8), pl.ds(row, 24)
        shifted_rows = pl.ds(pl.multiple_of(row + 8, 8), 8)
        values = [st[c, z, rows, :] for c in range(NC)]
        fluid = step_size * mk[z, rows, :].astype(f32)
        damping = sponge[z, rows, :]
        speeds, ratio = velocities(values)
        sixth = sixth_power(values[0])
        pressure = (sixth * values[0] - 1.0) * (1.0 / 7.0)
        for c in range(NC):
            flow = values[3] if c == 0 else values[c] * speeds[2]
            if c == 3:
                flow = flow + pressure
            near_x, wide_x = shifted_x(flow, lane)
            near_y, wide_y = shifted_y(fy[c, z, tall, :])
            near = (fz[c, z + 3, rows, :] - fz[c, z + 1, rows, :]) + near_y + near_x
            wide = (fz[c, z + 4, rows, :] - fz[c, z, rows, :]) + wide_y + wide_x
            value = values[c]
            next_ref[c, z, rows, :] = value - fluid * central(near, wide) - damping * (value - far_state[c])
        total = [(1.0 - damping) * sd[c, z, rows, :] for c in range(NC)]
        vector = []
        for c in range(NC):
            near = w[c, z + 3, shifted_rows, :] - w[c, z + 1, shifted_rows, :]
            wide = w[c, z + 4, shifted_rows, :] - w[c, z, shifted_rows, :]
            vector.append(central(near, wide))
        total = transposed(speeds, ratio, sixth, vector, 0, total)
        vector = [central(*shifted_y(w[c, z + 2, tall, :])) for c in range(NC)]
        total = transposed(speeds, ratio, sixth, vector, 1, total)
        vector = [central(*shifted_x(w[c, z + 2, shifted_rows, :], lane)) for c in range(NC)]
        total = transposed(speeds, ratio, sixth, vector, 2, total)
        square = carry
        for c in range(NC):
            grad_ref[c, z, rows, :] = total[c]
            square = square + total[c] * total[c]
        return square

    for kind, number in PASS_ON[-1]:
        relay(kind, number)

    def layer_cells(z, carry):
        square = lax.fori_loop(z * tiles, (z + 1) * tiles, cells, carry)

        @pl.when(z == CZ - 1)
        def _():
            send_z(1, F_LATE, (True,))

        for layer, planes in PASS_ON.items():
            if layer < 0 or layer >= CZ:
                continue

            @pl.when(z == layer)
            def _():
                for kind, number in planes:
                    relay(kind, number)

        return jnp.where((z >= 2) & (z < CZ - 2), square, carry)

    squares = lax.fori_loop(0, CZ, layer_cells, jnp.zeros((8, NX), f32))

    for side, there in ((0, has_down), (1, has_up)):
        planes = pl.ds(side * 20, 10)

        @pl.when(there)
        def _():
            wait_bytes(land.at[planes], arrive_sem.at[W_SEM + side])

        @pl.when(jnp.logical_not(there))
        def _():
            land[planes] = jnp.zeros((20 // 2, NY, NX), f32)

    def ends_cells(t, square):
        rows = pl.ds(pl.multiple_of(t * 8, 8), 8)
        for side in range(2):
            outer = [land[side * 20 + 2 * c + side, rows, :] for c in range(NC)]
            inner = [land[side * 20 + 2 * c + 1 - side, rows, :] for c in range(NC)]
            sign = -1.0 if side == 0 else 1.0
            edge, second = (0, 1) if side == 0 else (7, 6)
            cases = (
                (edge, [h1 * (sign * 8.0 / 12.0) - h2 * (sign / 12.0) for h1, h2 in zip(inner, outer)]),
                (second, [h1 * (-sign / 12.0) for h1 in inner]),
            )
            for z, vector in cases:
                values = [st[c, z, rows, :] for c in range(NC)]
                speeds, ratio = velocities(values)
                total = [grad_ref[c, z, rows, :] for c in range(NC)]
                total = transposed(speeds, ratio, sixth_power(values[0]), vector, 0, total)
                for c in range(NC):
                    grad_ref[c, z, rows, :] = total[c]
                    square = square + total[c] * total[c]
        return square

    squares = lax.fori_loop(0, tiles, ends_cells, squares)

    def flux_ends(low, high):
        for c in range(NC):
            for side, there in ((0, low), (1, high)):
                first = side * 20 + 10 + 2 * c

                @pl.when(there)
                def _():
                    wait_bytes(land.at[pl.ds(first, 2)], arrive_sem.at[F_SEM + side * NC + c])
                    outer, inner = land[first + side], land[first + 1 - side]
                    sign = -1.0 if side == 0 else 1.0
                    edge, second = (0, 1) if side == 0 else (7, 6)
                    cases = (
                        (edge, inner * (sign * 8.0 / 12.0) - outer * (sign / 12.0)),
                        (second, inner * (-sign / 12.0)),
                    )
                    for z, change in cases:
                        next_ref[c, z] = next_ref[c, z] - step_size * mk[z].astype(f32) * change

    running = squares[:, :128] + squares[:, 128:]
    sends = []
    for number, (place, others) in enumerate(groups):
        size, start = STAGE_SIZE[number], STAGE_START[number]
        parts[start + place] = running
        for to_z, to_y in others:
            pltpu.make_async_remote_copy(
                src_ref=parts.at[start + place],
                dst_ref=parts.at[start + place],
                send_sem=sum_send.at[number],
                recv_sem=sum_arrive.at[number],
                device_id=(to_z, to_y),
                device_id_type=MESH,
            ).start()
        for planes in PASS_ON[CZ + number]:
            relay(*planes)
        if number == 1:
            flux_ends(has_down & jnp.logical_not(down_corner), has_up & jnp.logical_not(up_corner))
        whole = parts.at[pl.ds(start, size - 1)]
        wait_bytes(whole, sum_arrive.at[number])
        running = parts[start]
        for other in range(1, size):
            running = running + parts[start + other]
        sends.append((whole, sum_send.at[number]))
    count = 1.0 * NC * CZ * NY * NX * 256
    gain_ref[...] = jnp.sqrt(jnp.broadcast_to(jnp.sum(running, keepdims=True), (8, 128)) / count + 1e-06)

    flux_ends(down_corner, up_corner)

    @pl.when(has_up)
    def _():
        wait_bytes(land.at[pl.ds(0, 20)], up_sem.at[0])

    @pl.when(has_down)
    def _():
        wait_bytes(land.at[pl.ds(0, 20)], down_sem.at[0])

    @pl.when(up_relay | down_relay)
    def _():
        wait_bytes(land.at[pl.ds(0, RELAYED)], forward_sem.at[0])

    for kind in range(2):

        @pl.when(has_right)
        def _():
            y_copy(kind, True).wait_send()

        @pl.when(has_left)
        def _():
            y_copy(kind, False).wait_send()

    for whole, sem in sends:
        wait_bytes(whole, sem)


def finish_kernel(next_vmem, grad_vmem, gain_vmem, next_ref, direction_ref, gain_ref, scaled, sems):
    copies = []
    inverse = jnp.broadcast_to(1.0 / gain_vmem[0:1, 0:1], (NY, NX))
    for c in range(NC):
        copies.append(pltpu.make_async_copy(next_vmem.at[c], next_ref.at[c], sems.at[c]))
        copies[-1].start()
    gain_ref[...] = gain_vmem[0:1, 0:1]
    for c in range(NC):

        def scale(z, carry):
            scaled[c, z] = grad_vmem[c, z] * inverse
            return carry

        lax.fori_loop(0, CZ, scale, 0)
        copies.append(pltpu.make_async_copy(scaled.at[c], direction_ref.at[c], sems.at[NC + c]))
        copies[-1].start()
    for copy in copies:
        copy.wait()


def local(state, adjoint_seed, fluid_mask, boundary_codes):
    block = (NC, CZ, NY, NX)
    inside = [pl.BlockSpec(memory_space=pltpu.VMEM)] * 3
    state_next, gradient, gain = pl.pallas_call(
        exchange_kernel,
        out_shape=[pltpu.VMEM(block, f32), pltpu.VMEM(block, f32), pltpu.VMEM((8, 128), f32)],
        in_specs=[pl.BlockSpec(memory_space=pltpu.HBM)] * 4,
        out_specs=inside,
        scratch_shapes=[
            pltpu.VMEM(block, f32),
            pltpu.VMEM(block, f32),
            pltpu.VMEM((CZ, NY, NX), jnp.int32),
            pltpu.VMEM((CZ, NY), jnp.int32),
            pltpu.VMEM((CZ, NY, NX), f32),
            pltpu.VMEM((NC, CZ + 4, NY + 16, NX), f32),
            pltpu.VMEM((NC, CZ + 4, NY, NX), f32),
            pltpu.VMEM((NC, CZ, NY + 16, NX), f32),
            pltpu.VMEM((RELAY_SLOT + RELAYED, NY, NX), f32),
            pltpu.VMEM((2, 2, NC, 2, 8, NX), f32),
            pltpu.VMEM((2, 2, NC, 2, 8, NX), f32),
            pltpu.VMEM((32, 8, 128), f32),
            pltpu.SemaphoreType.DMA((8,)),
            pltpu.SemaphoreType.DMA((1,)),
            pltpu.SemaphoreType.DMA((1,)),
            pltpu.SemaphoreType.DMA((R_SEM + RELAYED,)),
            pltpu.SemaphoreType.DMA((1,)),
            pltpu.SemaphoreType.DMA((2, 2)),
            pltpu.SemaphoreType.DMA((2, 2)),
            pltpu.SemaphoreType.DMA((2,)),
            pltpu.SemaphoreType.DMA((2,)),
        ],
        compiler_params=pltpu.CompilerParams(
            collective_id=0, has_side_effects=True, vmem_limit_bytes=40 * 1024 * 1024
        ),
    )(*[pltpu.with_memory_space_constraint(each, pltpu.HBM) for each in (state, adjoint_seed, fluid_mask, boundary_codes)])
    state_next, direction, gain = pl.pallas_call(
        finish_kernel,
        out_shape=[
            jax.ShapeDtypeStruct(block, f32),
            jax.ShapeDtypeStruct(block, f32),
            jax.ShapeDtypeStruct((1, 1), f32),
        ],
        in_specs=inside,
        out_specs=[
            pl.BlockSpec(memory_space=pl.ANY),
            pl.BlockSpec(memory_space=pl.ANY),
            pl.BlockSpec(memory_space=pltpu.VMEM),
        ],
        scratch_shapes=[pltpu.VMEM(block, f32), pltpu.SemaphoreType.DMA((2 * NC,))],
        compiler_params=pltpu.CompilerParams(vmem_limit_bytes=16 * 1024 * 1024),
    )(state_next, gradient, gain)
    return state_next, direction, gain.reshape(())


def solution(mesh):
    placed = (
        P(None, "gz", "gy", None),
        P(None, "gz", "gy", None),
        P("gz", "gy", None),
        P("gz", "gy"),
    )
    return jax.shard_map(
        local,
        mesh=mesh,
        in_specs=placed,
        out_specs=(P(None, "gz", "gy", None), P(None, "gz", "gy", None), P()),
        check_vma=False,
    )
```
